32 devices in a mesh: dp: 8 (over z, y), tensor: 4 (over x, core).
Axes of the slice: x: 2, y: 2, z: 4, core: 2. Of those that a mesh axis runs over, the one named last changes fastest.
Arguments:
- out_grad: bfloat16 [4096, 4096], P(('dp', 'tensor')), may hold values from -6 to 6
- attn_out: bfloat16 [4096, 4096], P('dp', 'tensor'), may hold values from -0.25 to 0.25
- o_weight: bfloat16 [4096, 4096], P('dp', 'tensor'), may hold values from -0.09375 to 0.09375
Outputs:
- attn_grad: bfloat16 [4096, 4096], P('dp', 'tensor')
- weight_grad: float32 [4096, 4096], P('dp', 'tensor')
The draws below stay inside these ranges and needn't reach their ends.
All inputs are finite; a program needn't handle non-finite values.
Results may differ from the reference program's by a relative error of at most 0.001.
Values may be sent and summed in bfloat16 or wider, within the bound.
A program may use at most 64 MiB of HBM per device.

```python
import jax
import jax.numpy as jnp

D = 4096
TOK_DEV = 128
HQ = 4096
TOKENS = 4096
N_DP = 8
N_TENSOR = 4


def raised(result, rng, source, target, blocks, factor):
    def block_of(dim):
        return (jnp.arange(result.shape[dim]) // (result.shape[dim] // blocks)).reshape((-1,) + (1,) * (result.ndim - 1 - dim))

    first = jax.random.permutation(rng, blocks)[block_of(target)]
    far = (block_of(target) + blocks // 2) % blocks
    return jnp.where((block_of(source) == first) | (block_of(source) == far), factor * result, result)


def levels(rng, extent, cuts, least, top_value):
    gain, own = 1.0, jax.random.fold_in(rng, 6)
    for axis_at, shards_of in cuts:
        steps = jnp.exp(jax.random.uniform(jax.random.fold_in(own, axis_at), (shards_of,), jnp.float32, least / len(cuts), top_value / len(cuts)))
        gain = gain * jnp.repeat(steps, extent[axis_at] // shards_of).reshape([-1 if axis == axis_at else 1 for axis in range(len(extent))])
    return gain


def bell_draw(own_key, shape, spread, bound, shards=(), dtype=jnp.bfloat16):
    values = spread * jax.random.normal(own_key, shape, jnp.float32)
    if shards:
        values = values * levels(own_key, shape, shards, -0.22, 0.18)
    return jnp.clip(values, -bound, bound).astype(dtype)


def noise_with(key, dims, spread, most, split, heavy, kind=jnp.bfloat16):
    drawn = spread * jax.random.normal(key, dims, jnp.float32)
    if split:
        drawn = drawn * levels(key, dims, split, -0.22, 0.18)
    return jnp.clip(raised(drawn, jax.random.fold_in(key, 3), *heavy), -most, most).astype(kind)


def setup_inputs(seed: int = 0) -> dict:
    arg_keys = jax.random.split(jax.random.key(seed), 4)
    return {
        "out_grad": noise_with(arg_keys[0], (TOKENS, D), 1.0, 6.0, ((0, 32),), (0, 1, 32, 2.75)),
        "attn_out": bell_draw(arg_keys[1], (TOKENS, HQ), ((TOK_DEV * N_TENSOR * N_DP) ** -0.5), 0.25, ((0, 8), (1, 4))),
        "o_weight": bell_draw(arg_keys[2], (D, HQ), HQ ** -0.5, 0.09375, ((0, 8), (1, 4))),
    }


def reference(out_grad, attn_out, o_weight):
    attn_grad = jnp.dot(out_grad, o_weight, preferred_element_type=jnp.float32).astype(jnp.bfloat16)
    weight_grad = jnp.dot(out_grad.T, attn_out, preferred_element_type=jnp.float32)
    return attn_grad, weight_grad
```

```python
import functools

import jax
import jax.numpy as jnp
from jax import lax
from jax.experimental import pallas as pl
from jax.experimental.pallas import tpu as pltpu
from jax.sharding import PartitionSpec as P

MESH = pl.DeviceIdType.MESH
CHUNK = 256


def kernel(n_dp, n_t, g_ref, a_ref, w_ref, attn_ref, wg_ref,
           G, A, W, up, down, acc, attn_send, attn_recv, wg_send, wg_recv,
           g_ssem, g_rsem, w_ssem, w_rsem, rs_ssem, rs_rsem, p_ssem, p_rsem):
    L, nx = n_dp // 2, n_t // 2
    T, S, R = g_ref.shape[0], a_ref.shape[0], w_ref.shape[0]
    H = a_ref.shape[1] // 2
    FB = 2 * R
    Q = FB // CHUNK
    K = 2 * S
    d, t = lax.axis_index("dp"), lax.axis_index("tensor")
    z, y = d // 2, d % 2
    x, c = t // 2, t % 2
    oy = 1 - y
    pair, core = (d + 1 - 2 * y, t), (d, t + 1 - 2 * c)
    above, below = (d + 2, t), (d - 2, t)
    has_above, has_below = z < L - 1, z > 0

    def beside(k):
        return (d, lax.rem(x + k, nx) * 2 + c)

    def cols(half):
        return pl.ds(pl.multiple_of(half * H, H), H)

    def copy(src, dst, ssem, rsem, to):
        return pltpu.make_async_remote_copy(
            src_ref=src, dst_ref=dst, send_sem=ssem, recv_sem=rsem, device_id=to, device_id_type=MESH)

    barrier = pltpu.get_barrier_semaphore()
    for other in [pair, core] + [beside(k) for k in range(1, nx)]:
        pl.semaphore_signal(barrier, inc=1, device_id=other, device_id_type=MESH)

    @pl.when(has_above)
    def _():
        pl.semaphore_signal(barrier, inc=1, device_id=above, device_id_type=MESH)

    @pl.when(has_below)
    def _():
        pl.semaphore_signal(barrier, inc=1, device_id=below, device_id_type=MESH)

    order = [v for s in range((L + 1) // 2) for v in ([L - 1 - s, s] if s != L - 1 - s else [s])]

    def block_at(p):
        return jnp.where(z < (L + 1) // 2, order[p], L - 1 - order[p])

    def g_slot(b, yy, xx, cc):
        row = pl.multiple_of((yy * n_t + xx * 2 + cc) * T, T)
        return G.at[b, pl.ds(row, T), :]

    def g_copy(p, slot, s_idx, r_idx, to):
        return copy(slot, slot, g_ssem.at[p, s_idx], g_rsem.at[p, r_idx], to)

    def xm(m):
        return lax.rem(x + m, nx)

    def g_own(p):
        b = block_at(p)
        slot = g_slot(b, y, x, c)
        slot[...] = g_ref[:, pl.ds(pl.multiple_of(b * FB, FB), FB)]
        g_copy(p, slot, 0, 0, pair).start()
        for k in range(1, nx):
            g_copy(p, slot, k, nx - k, beside(k)).start()
        g_copy(p, slot, 2 * nx - 1, 2 * nx - 1, core).start()

    def to_core(p, slot, j):
        g_copy(p, slot, 2 * nx - 1 + j, 2 * nx - 1 + j, core).start()

    def g_arrived(p, slot, r_idx):
        g_copy(p, slot, r_idx, r_idx, core).wait_recv()

    def g_from_pair(p):
        slot = g_slot(block_at(p), oy, x, c)
        g_arrived(p, slot, 0)
        for k in range(1, nx):
            g_copy(p, slot, nx - 1 + k, nx - 1 + nx - k, beside(k)).start()
        to_core(p, slot, nx)

    def g_rest(p):
        b = block_at(p)
        for m in range(1, nx):
            slot = g_slot(b, y, xm(m), c)
            g_arrived(p, slot, m)
            to_core(p, slot, m)
        for m in range(1, nx):
            slot = g_slot(b, oy, xm(m), c)
            g_arrived(p, slot, nx - 1 + m)
            to_core(p, slot, nx + m)
        for yy in range(2):
            for m in range(nx):
                slot = g_slot(b, y if yy == 0 else oy, xm(m), 1 - c)
                g_arrived(p, slot, 2 * nx - 1 + yy * nx + m)

    def g_sent(p):
        slot = g_slot(block_at(p), y, x, c)
        for i in range(4 * nx - 1):
            g_copy(p, slot, i, i, core).wait_send()

    def w_slot(b, yy):
        return W.at[b, pl.ds(pl.multiple_of(yy * R, R), R), :]

    def w_copy(b, yy, way, to):
        slot = w_slot(b, yy)
        return copy(slot, slot, w_ssem.at[way, b * 2 + yy], w_rsem.at[b * 2 + yy], to)

    def w_spread(b, yy, upward, downward):
        if upward:
            @pl.when(has_above)
            def _():
                w_copy(b, yy, 0, above).start()
        if downward:
            @pl.when(has_below)
            def _():
                w_copy(b, yy, 1, below).start()

    def a_swap(buf):
        return copy(a_ref.at[:, cols(oy)], buf.at[pl.ds(pl.multiple_of(y * S, S), S), :],
                    p_ssem.at[0], p_rsem.at[0], pair)

    def w_swap():
        return copy(w_ref.at[:, cols(oy)], w_slot(z, y), p_ssem.at[1], w_rsem.at[d], pair)

    def attn_block(b):
        def rows(i, _):
            r = pl.ds(pl.multiple_of(i * 256, 256), 256)
            acc[r, :] += jnp.dot(G[b, r, :], W[b], preferred_element_type=jnp.float32)
            return 0
        lax.fori_loop(0, K // 256, rows, 0)

    def w_wave(h):
        @pl.when(z - h >= 0)
        def _():
            for yy in range(2):
                w_copy(z - h, yy, 0, above).wait_recv()
                w_spread(z - h, yy, True, False)

        @pl.when(z + h <= L - 1)
        def _():
            for yy in range(2):
                w_copy(z + h, yy, 1, below).wait_recv()
                w_spread(z + h, yy, False, True)

        @pl.when(z - h >= 0)
        def _():
            attn_block(z - h)

        @pl.when(z + h <= L - 1)
        def _():
            attn_block(z + h)

    def rs_rows(q):
        return pl.ds(pl.multiple_of(q * CHUNK, CHUNK), CHUNK)

    def rs_copy(buf, way, b, q, to):
        slot = buf.at[b, rs_rows(q), :]
        return copy(slot, slot, rs_ssem.at[way, b, q], rs_rsem.at[way, b, q], to)

    def part(b, q):
        return lax.dot_general(G[b, :, rs_rows(q)], A[...], (((0,), (0,)), ((), ())),
                               preferred_element_type=jnp.float32)

    def rs_step(buf, way, b, q, has_before, to):
        buf_part = part(b, q)

        @pl.when(has_before)
        def _():
            rs_copy(buf, way, b, q, to).wait_recv()
            buf[b, rs_rows(q), :] += buf_part

        @pl.when(jnp.logical_not(has_before))
        def _():
            buf[b, rs_rows(q), :] = buf_part

        rs_copy(buf, way, b, q, to).start()

    def rs_both(s, q):
        @pl.when(L - 1 - s > z)
        def _():
            rs_step(up, 0, L - 1 - s, q, has_below, above)

        @pl.when(s < z)
        def _():
            rs_step(down, 1, s, q, has_above, below)

    def rs_stage(s):
        def one(q, _):
            rs_both(s, q)
            return 0
        lax.fori_loop(0, Q, one, 0)

    acc[...] = jnp.zeros_like(acc)
    A[pl.ds(pl.multiple_of(y * S, S), S), :] = a_ref[:, cols(y)]
    w_slot(z, y)[...] = w_ref[:, cols(y)]
    pl.semaphore_wait(barrier, 1 + nx + has_above.astype(jnp.int32) + has_below.astype(jnp.int32))

    g_own(0)
    w_spread(z, y, True, True)
    a_swap(A).start()
    g_from_pair(0)
    w_swap().start()
    if L > 1:
        g_own(1)
    g_rest(0)
    a_swap(A).wait_recv()
    at_end = jnp.logical_or(z == 0, z == L - 1)

    @pl.when(at_end)
    def _():
        rs_stage(0)

    w_copy(z, oy, 0, above).wait_recv()
    w_spread(z, oy, True, True)
    for p in range(1, L):
        g_from_pair(p)
        if p + 1 < L:
            g_own(p + 1)
        g_rest(p)

    @pl.when(jnp.logical_not(at_end))
    def _():
        rs_stage(0)

    attn_block(z)
    for s in range(1, L):
        rs_stage(s)
        w_wave(s)

    other_rows = pl.ds(pl.multiple_of(oy * S, S), S)
    own_rows = pl.ds(pl.multiple_of(y * S, S), S)
    attn_send[...] = acc[other_rows, :].astype(attn_send.dtype)
    attn_back = copy(attn_send, attn_recv, p_ssem.at[2], p_rsem.at[2], pair)
    attn_back.start()
    attn_ref[:, cols(y)] = acc[own_rows, :].astype(attn_ref.dtype)

    def wg_copy(i):
        r = rs_rows(i)
        return copy(wg_send.at[r, :], wg_recv.at[r, :], p_ssem.at[3 + i], p_rsem.at[3 + i], pair)

    def last(i, _):
        half = Q // 2
        q = lax.rem(i + oy * half, Q)
        total = part(z, q)
        acc[rs_rows(0), :] = total

        @pl.when(has_below)
        def _():
            rs_copy(up, 0, z, q, above).wait_recv()
            acc[rs_rows(0), :] += up[z, rs_rows(q), :]

        @pl.when(has_above)
        def _():
            rs_copy(down, 1, z, q, below).wait_recv()
            acc[rs_rows(0), :] += down[z, rs_rows(q), :]

        @pl.when(i < half)
        def _():
            wg_send[rs_rows(i), :] = acc[rs_rows(0), :]
            wg_copy(i).start()

        @pl.when(i >= half)
        def _():
            wg_ref[rs_rows(i - half), cols(y)] = acc[rs_rows(0), :]
        return 0

    lax.fori_loop(0, Q, last, 0)
    attn_back.wait_recv()
    attn_ref[:, cols(oy)] = attn_recv[...]

    def back(i, _):
        wg_copy(i).wait_recv()
        wg_ref[rs_rows(i), cols(oy)] = wg_recv[rs_rows(i), :]
        wg_copy(i).wait_send()
        return 0

    lax.fori_loop(0, Q // 2, back, 0)

    attn_back.wait_send()
    a_swap(A).wait_send()
    w_swap().wait_send()
    for p in range(L):
        g_sent(p)

    def w_sent(b, _):
        for yy in range(2):
            @pl.when(jnp.logical_and(has_above, b <= z))
            def _():
                w_copy(b, yy, 0, above).wait_send()

            @pl.when(jnp.logical_and(has_below, b >= z))
            def _():
                w_copy(b, yy, 1, below).wait_send()

        def chunk(q, _):
            @pl.when(b > z)
            def _():
                rs_copy(up, 0, b, q, above).wait_send()

            @pl.when(b < z)
            def _():
                rs_copy(down, 1, b, q, below).wait_send()
            return 0
        lax.fori_loop(0, Q, chunk, 0)
        return 0

    lax.fori_loop(0, L, w_sent, 0)


def solution(mesh):
    n_dp, n_t = mesh.shape["dp"], mesh.shape["tensor"]
    L, nx = n_dp // 2, n_t // 2

    def body(out_grad, attn_out, o_weight):
        S, C = attn_out.shape
        R = o_weight.shape[0]
        H, FB, K = C // 2, 2 * R, 2 * S
        Q = FB // CHUNK
        dma = pltpu.SemaphoreType.DMA
        bf16, f32 = jnp.bfloat16, jnp.float32
        vmem = pl.BlockSpec(memory_space=pltpu.VMEM)
        return pl.pallas_call(
            functools.partial(kernel, n_dp, n_t),
            out_shape=(jax.ShapeDtypeStruct((S, C), bf16), jax.ShapeDtypeStruct((R, C), f32)),
            in_specs=[vmem] * 3,
            out_specs=(vmem, vmem),
            scratch_shapes=[
                pltpu.VMEM((L, K, FB), bf16),
                pltpu.VMEM((K, H), bf16),
                pltpu.VMEM((L, FB, H), bf16),
                pltpu.VMEM((L, FB, H), f32),
                pltpu.VMEM((L, FB, H), f32),
                pltpu.VMEM((K, H), f32),
                pltpu.VMEM((S, H), bf16),
                pltpu.VMEM((S, H), bf16),
                pltpu.VMEM((R, H), f32),
                pltpu.VMEM((R, H), f32),
                dma((L, 4 * nx - 1)),
                dma((L, 4 * nx - 1)),
                dma((2, n_dp)),
                dma((n_dp,)),
                dma((2, L, Q)),
                dma((2, L, Q)),
                dma((3 + Q // 2,)),
                dma((3 + Q // 2,)),
            ],
            compiler_params=pltpu.CompilerParams(
                collective_id=0, has_side_effects=True, vmem_limit_bytes=60 * 1024 * 1024),
            cost_estimate=pl.CostEstimate(
                flops=4 * K * FB * L * H, bytes_accessed=8 * R * C, transcendentals=0),
        )(out_grad, attn_out, o_weight)

    return jax.shard_map(
        body,
        mesh=mesh,
        in_specs=(P(("dp", "tensor"), None), P("dp", "tensor"), P("dp", "tensor")),
        out_specs=(P("dp", "tensor"), P("dp", "tensor")),
        check_vma=False,
    )
```

```python
import functools

import jax
import jax.numpy as jnp
from jax import lax
from jax.experimental import pallas as pl
from jax.experimental.pallas import tpu as pltpu
from jax.sharding import PartitionSpec as P

MESH = pl.DeviceIdType.MESH
CHUNK = 256


def kernel(n_dp, n_t, g_ref, a_ref, w_ref, attn_ref, wg_ref,
           G, A, W, up, down, acc, attn_send, attn_recv, wg_send, wg_recv,
           g_ssem, g_rsem, w_ssem, w_rsem, rs_ssem, rs_rsem, p_ssem, p_rsem):
    L, nx = n_dp // 2, n_t // 2
    T, S, R = g_ref.shape[0], a_ref.shape[0], w_ref.shape[0]
    H = a_ref.shape[1] // 2
    FB = 2 * R
    Q = FB // CHUNK
    K = 2 * S
    d, t = lax.axis_index("dp"), lax.axis_index("tensor")
    z, y = d // 2, d % 2
    x, c = t // 2, t % 2
    oy = 1 - y
    pair, core = (d + 1 - 2 * y, t), (d, t + 1 - 2 * c)
    above, below = (d + 2, t), (d - 2, t)
    has_above, has_below = z < L - 1, z > 0

    def beside(k):
        return (d, lax.rem(x + k, nx) * 2 + c)

    def cols(half):
        return pl.ds(pl.multiple_of(half * H, H), H)

    def copy(src, dst, ssem, rsem, to):
        return pltpu.make_async_remote_copy(
            src_ref=src, dst_ref=dst, send_sem=ssem, recv_sem=rsem, device_id=to, device_id_type=MESH)

    barrier = pltpu.get_barrier_semaphore()
    for other in [pair, core] + [beside(k) for k in range(1, nx)]:
        pl.semaphore_signal(barrier, inc=1, device_id=other, device_id_type=MESH)

    @pl.when(has_above)
    def _():
        pl.semaphore_signal(barrier, inc=1, device_id=above, device_id_type=MESH)

    @pl.when(has_below)
    def _():
        pl.semaphore_signal(barrier, inc=1, device_id=below, device_id_type=MESH)

    order = [v for s in range((L + 1) // 2) for v in ([L - 1 - s, s] if s != L - 1 - s else [s])]

    def block_at(p):
        return jnp.where(z < (L + 1) // 2, order[p], L - 1 - order[p])

    def g_slot(b, yy, xx, cc):
        row = pl.multiple_of((yy * n_t + xx * 2 + cc) * T, T)
        return G.at[b, pl.ds(row, T), :]

    def g_copy(p, slot, s_idx, r_idx, to):
        return copy(slot, slot, g_ssem.at[p, s_idx], g_rsem.at[p, r_idx], to)

    def xm(m):
        return lax.rem(x + m, nx)

    def g_own(p):
        b = block_at(p)
        slot = g_slot(b, y, x, c)
        slot[...] = g_ref[:, pl.ds(pl.multiple_of(b * FB, FB), FB)]
        g_copy(p, slot, 0, 0, pair).start()
        for k in range(1, nx):
            g_copy(p, slot, k, nx - k, beside(k)).start()
        g_copy(p, slot, 2 * nx - 1, 2 * nx - 1, core).start()

    def to_core(p, slot, j):
        g_copy(p, slot, 2 * nx - 1 + j, 2 * nx - 1 + j, core).start()

    def g_arrived(p, slot, r_idx):
        g_copy(p, slot, r_idx, r_idx, core).wait_recv()

    def g_from_pair(p):
        slot = g_slot(block_at(p), oy, x, c)
        g_arrived(p, slot, 0)
        for k in range(1, nx):
            g_copy(p, slot, nx - 1 + k, nx - 1 + nx - k, beside(k)).start()
        to_core(p, slot, nx)

    def g_rest(p):
        b = block_at(p)
        for m in range(1, nx):
            slot = g_slot(b, y, xm(m), c)
            g_arrived(p, slot, m)
            to_core(p, slot, m)
        for m in range(1, nx):
            slot = g_slot(b, oy, xm(m), c)
            g_arrived(p, slot, nx - 1 + m)
            to_core(p, slot, nx + m)
        for yy in range(2):
            for m in range(nx):
                slot = g_slot(b, y if yy == 0 else oy, xm(m), 1 - c)
                g_arrived(p, slot, 2 * nx - 1 + yy * nx + m)

    def g_sent(p):
        slot = g_slot(block_at(p), y, x, c)
        for i in range(4 * nx - 1):
            g_copy(p, slot, i, i, core).wait_send()

    def w_slot(b, yy):
        return W.at[b, pl.ds(pl.multiple_of(yy * R, R), R), :]

    def w_copy(b, yy, way, to):
        slot = w_slot(b, yy)
        return copy(slot, slot, w_ssem.at[way, b * 2 + yy], w_rsem.at[b * 2 + yy], to)

    def w_spread(b, yy, upward, downward):
        if upward:
            @pl.when(has_above)
            def _():
                w_copy(b, yy, 0, above).start()
        if downward:
            @pl.when(has_below)
            def _():
                w_copy(b, yy, 1, below).start()

    def a_swap(buf):
        return copy(a_ref.at[:, cols(oy)], buf.at[pl.ds(pl.multiple_of(y * S, S), S), :],
                    p_ssem.at[0], p_rsem.at[0], pair)

    def w_swap():
        return copy(w_ref.at[:, cols(oy)], w_slot(z, y), p_ssem.at[1], w_rsem.at[d], pair)

    def attn_block(b):
        def rows(i, _):
            r = pl.ds(pl.multiple_of(i * 256, 256), 256)
            acc[r, :] += jnp.dot(G[b, r, :], W[b], preferred_element_type=jnp.float32)
            return 0
        lax.fori_loop(0, K // 256, rows, 0)

    def w_wave(h):
        @pl.when(z - h >= 0)
        def _():
            for yy in range(2):
                w_copy(z - h, yy, 0, above).wait_recv()
                w_spread(z - h, yy, True, False)

        @pl.when(z + h <= L - 1)
        def _():
            for yy in range(2):
                w_copy(z + h, yy, 1, below).wait_recv()
                w_spread(z + h, yy, False, True)

        @pl.when(z - h >= 0)
        def _():
            attn_block(z - h)

        @pl.when(z + h <= L - 1)
        def _():
            attn_block(z + h)

    def rs_rows(q):
        return pl.ds(pl.multiple_of(q * CHUNK, CHUNK), CHUNK)

    def rs_copy(buf, way, b, q, to):
        slot = buf.at[b, rs_rows(q), :]
        return copy(slot, slot, rs_ssem.at[way, b, q], rs_rsem.at[way, b, q], to)

    def part(b, q):
        return lax.dot_general(G[b, :, rs_rows(q)], A[...], (((0,), (0,)), ((), ())),
                               preferred_element_type=jnp.float32)

    def rs_step(buf, way, b, q, has_before, to):
        buf_part = part(b, q)

        @pl.when(has_before)
        def _():
            rs_copy(buf, way, b, q, to).wait_recv()
            buf[b, rs_rows(q), :] += buf_part

        @pl.when(jnp.logical_not(has_before))
        def _():
            buf[b, rs_rows(q), :] = buf_part

        rs_copy(buf, way, b, q, to).start()

    def perm(i):
        return lax.rem(i + oy * (Q // 2), Q)

    def rs_iter(i):
        ui, di = i - z, i - (L - 1 - z)
        uc, dc = jnp.maximum(ui, 0), jnp.maximum(di, 0)

        @pl.when(jnp.logical_and(ui >= 0, ui < (L - 1 - z) * Q))
        def _():
            rs_step(up, 0, L - 1 - uc // Q, perm(lax.rem(uc, Q)), has_below, above)

        @pl.when(jnp.logical_and(di >= 0, di < z * Q))
        def _():
            rs_step(down, 1, dc // Q, perm(lax.rem(dc, Q)), has_above, below)

    def rs_stage(s):
        def one(i, _):
            rs_iter(i)
            return 0
        lax.fori_loop(s * Q, (s + 1) * Q, one, 0)

    acc[...] = jnp.zeros_like(acc)
    A[pl.ds(pl.multiple_of(y * S, S), S), :] = a_ref[:, cols(y)]
    w_slot(z, y)[...] = w_ref[:, cols(y)]
    pl.semaphore_wait(barrier, 1 + nx + has_above.astype(jnp.int32) + has_below.astype(jnp.int32))

    g_own(0)
    w_spread(z, y, True, True)
    a_swap(A).start()
    g_from_pair(0)
    w_swap().start()
    if L > 1:
        g_own(1)
    g_rest(0)
    a_swap(A).wait_recv()
    at_end = jnp.logical_or(z == 0, z == L - 1)

    @pl.when(at_end)
    def _():
        rs_stage(0)

    w_copy(z, oy, 0, above).wait_recv()
    w_spread(z, oy, True, True)
    for p in range(1, L):
        g_from_pair(p)
        if p + 1 < L:
            g_own(p + 1)
        g_rest(p)

    @pl.when(jnp.logical_not(at_end))
    def _():
        rs_stage(0)

    attn_block(z)
    for s in range(1, L):
        w_wave(s)
        if s < L - 1:
            rs_stage(s)

    other_rows = pl.ds(pl.multiple_of(oy * S, S), S)
    own_rows = pl.ds(pl.multiple_of(y * S, S), S)
    attn_send[...] = acc[other_rows, :].astype(attn_send.dtype)
    attn_back = copy(attn_send, attn_recv, p_ssem.at[2], p_rsem.at[2], pair)
    attn_back.start()
    attn_ref[:, cols(y)] = acc[own_rows, :].astype(attn_ref.dtype)

    def wg_copy(i):
        r = rs_rows(i)
        return copy(wg_send.at[r, :], wg_recv.at[r, :], p_ssem.at[3 + i], p_rsem.at[3 + i], pair)

    def last(i, _):
        half = Q // 2
        q = perm(i)
        total = part(z, q)
        acc[rs_rows(0), :] = total

        @pl.when(has_below)
        def _():
            rs_copy(up, 0, z, q, above).wait_recv()
            acc[rs_rows(0), :] += up[z, rs_rows(q), :]

        @pl.when(has_above)
        def _():
            rs_copy(down, 1, z, q, below).wait_recv()
            acc[rs_rows(0), :] += down[z, rs_rows(q), :]

        @pl.when(i < half)
        def _():
            wg_send[rs_rows(i), :] = acc[rs_rows(0), :]
            wg_copy(i).start()

        @pl.when(i >= half)
        def _():
            wg_ref[rs_rows(i - half), cols(y)] = acc[rs_rows(0), :]
        return 0

    lax.fori_loop(0, Q, last, 0)
    attn_back.wait_recv()
    attn_ref[:, cols(oy)] = attn_recv[...]

    def back(i, _):
        wg_copy(i).wait_recv()
        wg_ref[rs_rows(i), cols(oy)] = wg_recv[rs_rows(i), :]
        wg_copy(i).wait_send()
        return 0

    lax.fori_loop(0, Q // 2, back, 0)

    attn_back.wait_send()
    a_swap(A).wait_send()
    w_swap().wait_send()
    for p in range(L):
        g_sent(p)

    def w_sent(b, _):
        for yy in range(2):
            @pl.when(jnp.logical_and(has_above, b <= z))
            def _():
                w_copy(b, yy, 0, above).wait_send()

            @pl.when(jnp.logical_and(has_below, b >= z))
            def _():
                w_copy(b, yy, 1, below).wait_send()

        def chunk(q, _):
            @pl.when(b > z)
            def _():
                rs_copy(up, 0, b, q, above).wait_send()

            @pl.when(b < z)
            def _():
                rs_copy(down, 1, b, q, below).wait_send()
            return 0
        lax.fori_loop(0, Q, chunk, 0)
        return 0

    lax.fori_loop(0, L, w_sent, 0)


def solution(mesh):
    n_dp, n_t = mesh.shape["dp"], mesh.shape["tensor"]
    L, nx = n_dp // 2, n_t // 2

    def body(out_grad, attn_out, o_weight):
        S, C = attn_out.shape
        R = o_weight.shape[0]
        H, FB, K = C // 2, 2 * R, 2 * S
        Q = FB // CHUNK
        dma = pltpu.SemaphoreType.DMA
        bf16, f32 = jnp.bfloat16, jnp.float32
        vmem = pl.BlockSpec(memory_space=pltpu.VMEM)
        return pl.pallas_call(
            functools.partial(kernel, n_dp, n_t),
            out_shape=(jax.ShapeDtypeStruct((S, C), bf16), jax.ShapeDtypeStruct((R, C), f32)),
            in_specs=[vmem] * 3,
            out_specs=(vmem, vmem),
            scratch_shapes=[
                pltpu.VMEM((L, K, FB), bf16),
                pltpu.VMEM((K, H), bf16),
                pltpu.VMEM((L, FB, H), bf16),
                pltpu.VMEM((L, FB, H), f32),
                pltpu.VMEM((L, FB, H), f32),
                pltpu.VMEM((K, H), f32),
                pltpu.VMEM((S, H), bf16),
                pltpu.VMEM((S, H), bf16),
                pltpu.VMEM((R, H), f32),
                pltpu.VMEM((R, H), f32),
                dma((L, 4 * nx - 1)),
                dma((L, 4 * nx - 1)),
                dma((2, n_dp)),
                dma((n_dp,)),
                dma((2, L, Q)),
                dma((2, L, Q)),
                dma((3 + Q // 2,)),
                dma((3 + Q // 2,)),
            ],
            compiler_params=pltpu.CompilerParams(
                collective_id=0, has_side_effects=True, vmem_limit_bytes=60 * 1024 * 1024),
            cost_estimate=pl.CostEstimate(
                flops=4 * K * FB * L * H, bytes_accessed=8 * R * C, transcendentals=0),
        )(out_grad, attn_out, o_weight)

    return jax.shard_map(
        body,
        mesh=mesh,
        in_specs=(P(("dp", "tensor"), None), P("dp", "tensor"), P("dp", "tensor")),
        out_specs=(P("dp", "tensor"), P("dp", "tensor")),
        check_vma=False,
    )
```

```python
import functools

import jax
import jax.numpy as jnp
from jax import lax
from jax.experimental import pallas as pl
from jax.experimental.pallas import tpu as pltpu
from jax.sharding import PartitionSpec as P

MESH = pl.DeviceIdType.MESH
CHUNK = 256


def sum_kernel(n_dp, n_t, g_ref, a_ref, w_ref, attn_ref, wg_ref,
           G, A, W, up, down, acc, attn_send, attn_recv, wg_send, wg_recv,
           g_ssem, g_rsem, w_ssem, w_rsem, rs_ssem, rs_rsem, p_ssem, p_rsem):
    L, nx = n_dp // 2, n_t // 2
    T, S, R = g_ref.shape[0], a_ref.shape[0], w_ref.shape[0]
    H = a_ref.shape[1] // 2
    FB = 2 * R
    Q = FB // CHUNK
    K = 2 * S
    d, t = lax.axis_index("dp"), lax.axis_index("tensor")
    z, y = d // 2, d % 2
    x, c = t // 2, t % 2
    oy = 1 - y
    pair, core = (d + 1 - 2 * y, t), (d, t + 1 - 2 * c)
    above, below = (d + 2, t), (d - 2, t)
    has_above, has_below = z < L - 1, z > 0

    def beside(k):
        return (d, lax.rem(x + k, nx) * 2 + c)

    def cols(half):
        return pl.ds(pl.multiple_of(half * H, H), H)

    def copy(src, dst, ssem, rsem, to):
        return pltpu.make_async_remote_copy(
            src_ref=src, dst_ref=dst, send_sem=ssem, recv_sem=rsem, device_id=to, device_id_type=MESH)

    barrier = pltpu.get_barrier_semaphore()
    for other in [pair, core] + [beside(k) for k in range(1, nx)]:
        pl.semaphore_signal(barrier, inc=1, device_id=other, device_id_type=MESH)

    @pl.when(has_above)
    def _():
        pl.semaphore_signal(barrier, inc=1, device_id=above, device_id_type=MESH)

    @pl.when(has_below)
    def _():
        pl.semaphore_signal(barrier, inc=1, device_id=below, device_id_type=MESH)

    order = [v for s in range((L + 1) // 2) for v in ([L - 1 - s, s] if s != L - 1 - s else [s])]

    def block_at(p):
        return jnp.where(z < (L + 1) // 2, order[p], L - 1 - order[p])

    def g_slot(b, yy, xx, cc):
        row = pl.multiple_of((yy * n_t + xx * 2 + cc) * T, T)
        return G.at[b, pl.ds(row, T), :]

    def g_copy(p, slot, s_idx, r_idx, to):
        return copy(slot, slot, g_ssem.at[p, s_idx], g_rsem.at[p, r_idx], to)

    def xm(m):
        return lax.rem(x + m, nx)

    def g_own(p):
        b = block_at(p)
        slot = g_slot(b, y, x, c)
        slot[...] = g_ref[:, pl.ds(pl.multiple_of(b * FB, FB), FB)]
        g_copy(p, slot, 0, 0, pair).start()
        for k in range(1, nx):
            g_copy(p, slot, k, nx - k, beside(k)).start()
        g_copy(p, slot, 2 * nx - 1, 2 * nx - 1, core).start()

    def to_core(p, slot, j):
        g_copy(p, slot, 2 * nx - 1 + j, 2 * nx - 1 + j, core).start()

    def g_arrived(p, slot, r_idx):
        g_copy(p, slot, r_idx, r_idx, core).wait_recv()

    def g_from_pair(p):
        slot = g_slot(block_at(p), oy, x, c)
        g_arrived(p, slot, 0)
        for k in range(1, nx):
            g_copy(p, slot, nx - 1 + k, nx - 1 + nx - k, beside(k)).start()
        to_core(p, slot, nx)

    def g_rest(p):
        b = block_at(p)
        for m in range(1, nx):
            slot = g_slot(b, y, xm(m), c)
            g_arrived(p, slot, m)
            to_core(p, slot, m)
        for m in range(1, nx):
            slot = g_slot(b, oy, xm(m), c)
            g_arrived(p, slot, nx - 1 + m)
            to_core(p, slot, nx + m)
        for yy in range(2):
            for m in range(nx):
                slot = g_slot(b, y if yy == 0 else oy, xm(m), 1 - c)
                g_arrived(p, slot, 2 * nx - 1 + yy * nx + m)

    def g_sent(p):
        slot = g_slot(block_at(p), y, x, c)
        for i in range(4 * nx - 1):
            g_copy(p, slot, i, i, core).wait_send()

    def w_slot(b, yy):
        return W.at[b, pl.ds(pl.multiple_of(yy * R, R), R), :]

    def w_copy(b, yy, way, to):
        slot = w_slot(b, yy)
        return copy(slot, slot, w_ssem.at[way, b * 2 + yy], w_rsem.at[b * 2 + yy], to)

    def w_spread(b, yy, upward, downward):
        if upward:
            @pl.when(has_above)
            def _():
                w_copy(b, yy, 0, above).start()
        if downward:
            @pl.when(has_below)
            def _():
                w_copy(b, yy, 1, below).start()

    def a_swap(buf):
        return copy(a_ref.at[:, cols(oy)], buf.at[pl.ds(pl.multiple_of(y * S, S), S), :],
                    p_ssem.at[0], p_rsem.at[0], pair)

    def w_swap():
        return copy(w_ref.at[:, cols(oy)], w_slot(z, y), p_ssem.at[1], w_rsem.at[d], pair)

    def attn_block(b):
        def rows(i, _):
            r = pl.ds(pl.multiple_of(i * 256, 256), 256)
            acc[r, :] += jnp.dot(G[b, r, :], W[b], preferred_element_type=jnp.float32)
            return 0
        lax.fori_loop(0, K // 256, rows, 0)

    def w_wave(h):
        @pl.when(z - h >= 0)
        def _():
            for yy in range(2):
                w_copy(z - h, yy, 0, above).wait_recv()
                w_spread(z - h, yy, True, False)

        @pl.when(z + h <= L - 1)
        def _():
            for yy in range(2):
                w_copy(z + h, yy, 1, below).wait_recv()
                w_spread(z + h, yy, False, True)

        @pl.when(z - h >= 0)
        def _():
            attn_block(z - h)

        @pl.when(z + h <= L - 1)
        def _():
            attn_block(z + h)

    def rs_rows(q):
        return pl.ds(pl.multiple_of(q * CHUNK, CHUNK), CHUNK)

    def rs_copy(buf, way, b, q, to):
        slot = buf.at[b, rs_rows(q), :]
        return copy(slot, slot, rs_ssem.at[way, b, q], rs_rsem.at[way, b, q], to)

    def part(b, q):
        return lax.dot_general(G[b, :, rs_rows(q)], A[...], (((0,), (0,)), ((), ())),
                               preferred_element_type=jnp.float32)

    def rs_step(buf, way, b, q, has_before, to):
        buf_part = part(b, q)

        @pl.when(has_before)
        def _():
            rs_copy(buf, way, b, q, to).wait_recv()
            buf[b, rs_rows(q), :] += buf_part

        @pl.when(jnp.logical_not(has_before))
        def _():
            buf[b, rs_rows(q), :] = buf_part

        rs_copy(buf, way, b, q, to).start()

    def perm(i):
        return lax.rem(i + oy * (Q // 2), Q)

    def rs_iter(i):
        ui, di = i - z, i - (L - 1 - z)
        uc, dc = jnp.maximum(ui, 0), jnp.maximum(di, 0)

        @pl.when(jnp.logical_and(ui >= 0, ui < (L - 1 - z) * Q))
        def _():
            rs_step(up, 0, L - 1 - uc // Q, perm(lax.rem(uc, Q)), has_below, above)

        @pl.when(jnp.logical_and(di >= 0, di < z * Q))
        def _():
            rs_step(down, 1, dc // Q, perm(lax.rem(dc, Q)), has_above, below)

    def rs_stage(s):
        def one(i, _):
            rs_iter(i)
            return 0
        lax.fori_loop(s * Q, (s + 1) * Q, one, 0)

    acc[...] = jnp.zeros_like(acc)
    A[pl.ds(pl.multiple_of(y * S, S), S), :] = a_ref[:, cols(y)]
    w_slot(z, y)[...] = w_ref[:, cols(y)]
    pl.semaphore_wait(barrier, 1 + nx + has_above.astype(jnp.int32) + has_below.astype(jnp.int32))

    g_own(0)
    w_spread(z, y, True, True)
    a_swap(A).start()
    g_from_pair(0)
    w_swap().start()
    if L > 1:
        g_own(1)
    g_rest(0)
    a_swap(A).wait_recv()
    at_end = jnp.logical_or(z == 0, z == L - 1)

    @pl.when(at_end)
    def _():
        rs_stage(0)

    w_copy(z, oy, 0, above).wait_recv()
    w_spread(z, oy, True, True)
    for p in range(1, L):
        g_from_pair(p)
        if p + 1 < L:
            g_own(p + 1)
        g_rest(p)

    @pl.when(jnp.logical_not(at_end))
    def _():
        rs_stage(0)

    attn_block(z)
    for s in range(1, L):
        w_wave(s)
        if s < L - 1:
            rs_stage(s)

    other_rows = pl.ds(pl.multiple_of(oy * S, S), S)
    own_rows = pl.ds(pl.multiple_of(y * S, S), S)
    attn_send[...] = acc[other_rows, :].astype(attn_send.dtype)
    attn_back = copy(attn_send, attn_recv, p_ssem.at[2], p_rsem.at[2], pair)
    attn_back.start()
    attn_ref[:, cols(y)] = acc[own_rows, :].astype(attn_ref.dtype)

    def wg_copy(i):
        r = rs_rows(i)
        return copy(wg_send.at[r, :], wg_recv.at[r, :], p_ssem.at[3 + i], p_rsem.at[3 + i], pair)

    def last(i, _):
        half = Q // 2
        q = perm(i)
        total = part(z, q)
        acc[rs_rows(0), :] = total

        @pl.when(has_below)
        def _():
            rs_copy(up, 0, z, q, above).wait_recv()
            acc[rs_rows(0), :] += up[z, rs_rows(q), :]

        @pl.when(has_above)
        def _():
            rs_copy(down, 1, z, q, below).wait_recv()
            acc[rs_rows(0), :] += down[z, rs_rows(q), :]

        @pl.when(i < half)
        def _():
            wg_send[rs_rows(i), :] = acc[rs_rows(0), :]
            wg_copy(i).start()

        @pl.when(i >= half)
        def _():
            wg_ref[rs_rows(i - half), cols(y)] = acc[rs_rows(0), :]
        return 0

    lax.fori_loop(0, Q, last, 0)
    attn_back.wait_recv()
    attn_ref[:, cols(oy)] = attn_recv[...]

    def back(i, _):
        wg_copy(i).wait_recv()
        wg_ref[rs_rows(i), cols(oy)] = wg_recv[rs_rows(i), :]
        wg_copy(i).wait_send()
        return 0

    lax.fori_loop(0, Q // 2, back, 0)

    attn_back.wait_send()
    a_swap(A).wait_send()
    w_swap().wait_send()
    for p in range(L):
        g_sent(p)

    def w_sent(b, _):
        for yy in range(2):
            @pl.when(jnp.logical_and(has_above, b <= z))
            def _():
                w_copy(b, yy, 0, above).wait_send()

            @pl.when(jnp.logical_and(has_below, b >= z))
            def _():
                w_copy(b, yy, 1, below).wait_send()

        def chunk(q, _):
            @pl.when(b > z)
            def _():
                rs_copy(up, 0, b, q, above).wait_send()

            @pl.when(b < z)
            def _():
                rs_copy(down, 1, b, q, below).wait_send()
            return 0
        lax.fori_loop(0, Q, chunk, 0)
        return 0

    lax.fori_loop(0, L, w_sent, 0)


def gather_kernel(n_t, g_ref, a_ref, w_ref, attn_ref, wg_ref,
                  G, GX, A, W, acc, attn_send, attn_recv, far, far_recv, wg_send, wg_recv,
                  g_ssem, g_rsem, z_ssem, z_rsem, w_ssem, w_rsem, a_ssem, a_rsem,
                  far_ssem, far_rsem, p_ssem, p_rsem):
    L, nx = 4, n_t // 2
    T, S, R = g_ref.shape[0], a_ref.shape[0], w_ref.shape[0]
    H = a_ref.shape[1] // 2
    FB = 2 * R
    Q = FB // CHUNK
    K = 2 * S
    half = Q // 2
    d, t = lax.axis_index("dp"), lax.axis_index("tensor")
    z, y = d // 2, d % 2
    x, c = t // 2, t % 2
    oy = 1 - y
    pair, core = (d + 1 - 2 * y, t), (d, t + 1 - 2 * c)
    above, below = (d + 2, t), (d - 2, t)
    has_above, has_below = z < L - 1, z > 0
    top = z // 2
    middle = jnp.logical_or(z == 1, z == 2)
    at_end = jnp.logical_not(middle)

    def layer(zz):
        return (zz * 2 + y, t)

    def beside(k):
        return (d, lax.rem(x + k, nx) * 2 + c)

    def cols(h):
        return pl.ds(pl.multiple_of(h * H, H), H)

    def copy(src, dst, ssem, rsem, to):
        return pltpu.make_async_remote_copy(
            src_ref=src, dst_ref=dst, send_sem=ssem, recv_sem=rsem, device_id=to, device_id_type=MESH)

    barrier = pltpu.get_barrier_semaphore()

    def greet(to):
        pl.semaphore_signal(barrier, inc=1, device_id=to, device_id_type=MESH)

    for other in [pair, core] + [beside(k) for k in range(1, nx)]:
        greet(other)
    pl.when(has_above)(lambda: greet(above))
    pl.when(has_below)(lambda: greet(below))
    pl.when(z < 2)(lambda: greet((d + 4, t)))
    pl.when(z >= 2)(lambda: greet((d - 4, t)))

    def g_slot(p, yy, xx, cc):
        return G.at[p, pl.ds(pl.multiple_of((yy * n_t + xx * 2 + cc) * T, T), T), :]

    def gx_slot(p, yy, xx, cc):
        return GX.at[p - L, pl.ds(pl.multiple_of((yy * n_t + xx * 2 + cc) * T, T), T), :]

    def g_copy(p, slot, s_idx, r_idx, to):
        return copy(slot, slot, g_ssem.at[p, s_idx], g_rsem.at[p, r_idx], to)

    def xm(m):
        return lax.rem(x + m, nx)

    def to_core(p, slot, j):
        g_copy(p, slot, 2 * nx - 1 + j, 2 * nx - 1 + j, core).start()

    def spread(p, at):
        slot = at(p, y, x, c)
        g_copy(p, slot, 0, 0, pair).start()
        for k in range(1, nx):
            g_copy(p, slot, k, nx - k, beside(k)).start()
        to_core(p, slot, 0)

    def arrived(p, slot, r_idx):
        g_copy(p, slot, r_idx, r_idx, core).wait_recv()

    def from_pair(p, at):
        slot = at(p, oy, x, c)
        arrived(p, slot, 0)
        for k in range(1, nx):
            g_copy(p, slot, nx - 1 + k, nx - 1 + nx - k, beside(k)).start()
        to_core(p, slot, nx)

    def rest(p, at):
        for m in range(1, nx):
            slot = at(p, y, xm(m), c)
            arrived(p, slot, m)
            to_core(p, slot, m)
        for m in range(1, nx):
            slot = at(p, oy, xm(m), c)
            arrived(p, slot, nx - 1 + m)
            to_core(p, slot, nx + m)
        for yy in range(2):
            for m in range(nx):
                arrived(p, at(p, y if yy == 0 else oy, xm(m), 1 - c), 2 * nx - 1 + yy * nx + m)

    def all_sent(p, at):
        for i in range(4 * nx - 1):
            g_copy(p, at(p, y, x, c), i, i, core).wait_send()

    def z_copy(h, j):
        return copy(g_slot(2 * h + j, y, x, c), gx_slot(L + z * 2 + j, y, x, c),
                    z_ssem.at[h * 2 + j], z_rsem.at[z * 2 + j], layer(1 + h))

    def z_all(act):
        for h in (0, 1):
            @pl.when(z != 1 + h)
            def _():
                for j in (0, 1):
                    act(z_copy(h, j))

    def extra_layer(e):
        o = jnp.where(e == 0, 0, e + 1)
        return jnp.where(z == 1, o, L - 1 - o)

    def z_arrived(zz, j):
        p = L + zz * 2 + j
        slot = gx_slot(p, y, x, c)
        copy(slot, slot, z_ssem.at[0], z_rsem.at[zz * 2 + j], core).wait_recv()
        spread(p, gx_slot)

    def extra(e):
        zz = extra_layer(e)
        for j in (0, 1):
            from_pair(L + zz * 2 + j, gx_slot)
            rest(L + zz * 2 + j, gx_slot)

    def unit(buf, b, yy, size):
        return buf.at[b, pl.ds(pl.multiple_of(yy * size, size), size), :]

    def w_copy(b, yy, way, to):
        slot = unit(W, b, yy, R)
        return copy(slot, slot, w_ssem.at[way, b * 2 + yy], w_rsem.at[b * 2 + yy], to)

    def a_copy(b, yy, way, to):
        slot = unit(A, b, yy, S)
        return copy(slot, slot, a_ssem.at[way, b * 2 + yy], a_rsem.at[b * 2 + yy], to)

    def a_up(b):
        return jnp.logical_and(z <= 1, b <= z)

    def a_down(b):
        return jnp.logical_and(z >= 2, b >= z)

    def a_spread(b, yy):
        pl.when(a_up(b))(lambda: a_copy(b, yy, 0, above).start())
        pl.when(a_down(b))(lambda: a_copy(b, yy, 1, below).start())

    def w_out(b, yy):
        pl.when(jnp.logical_and(z == 2, b <= z))(lambda: w_copy(b, yy, 0, above).start())
        pl.when(jnp.logical_and(z == 1, b >= z))(lambda: w_copy(b, yy, 1, below).start())

    def w_in(b, yy):
        pl.when(jnp.logical_and(z <= 1, b <= z))(lambda: w_copy(b, yy, 0, above).start())
        pl.when(jnp.logical_and(z >= 2, b >= z))(lambda: w_copy(b, yy, 1, below).start())

    def a_swap():
        return copy(a_ref.at[:, cols(oy)], unit(A, z, y, S), p_ssem.at[0], a_rsem.at[d], pair)

    def w_swap():
        return copy(w_ref.at[:, cols(oy)], unit(W, z, y, R), p_ssem.at[1], w_rsem.at[d], pair)

    def attn_block(b):
        def rows(i, _):
            r = pl.ds(pl.multiple_of(i * 256, 256), 256)
            acc[r, :] += jnp.dot(G[b, r, :], W[b], preferred_element_type=jnp.float32)
            return 0
        lax.fori_loop(0, K // 256, rows, 0)

    def w_wave(h):
        for b, ok in ((z - h, z - h >= 0), (z + h, z + h <= L - 1)):
            @pl.when(ok)
            def _():
                for yy in range(2):
                    w_copy(b, yy, 0, core).wait_recv()
                    pl.when(jnp.logical_and(has_above, b < z))(lambda: w_copy(b, yy, 0, above).start())
                    pl.when(jnp.logical_and(has_below, b > z))(lambda: w_copy(b, yy, 1, below).start())
        for b, ok in ((z - h, z - h >= 0), (z + h, z + h <= L - 1)):
            pl.when(ok)(lambda: attn_block(b))

    def a_wave(b):
        for yy in range(2):
            a_copy(b, yy, 0, core).wait_recv()
            a_spread(b, yy)

    def q_rows(q):
        return pl.ds(pl.multiple_of(q * CHUNK, CHUNK), CHUNK)

    def perm(i):
        return lax.rem(i + oy * half, Q)

    def part(g, a):
        return lax.dot_general(g, a, (((0,), (0,)), ((), ())), preferred_element_type=jnp.float32)

    def rows_of(b, q):
        total = part(G[b, :, q_rows(q)], A[z])
        for e in range(3):
            zz = extra_layer(e)
            total += part(GX[zz * 2 + b - 2 * top, :, q_rows(q)], A[zz])
        return total

    def far_copy(q):
        return copy(far.at[q_rows(q), :], far_recv.at[q_rows(q), :], far_ssem.at[q], far_rsem.at[q], layer(3 * top))

    def far_landed(q):
        return copy(far.at[q_rows(q), :], far_recv.at[q_rows(q), :], far_ssem.at[q], far_rsem.at[q], core)

    def make_far(i, _):
        q = perm(i)
        far[q_rows(q), :] = rows_of(3 * top, q)
        far_copy(q).start()
        return 0

    def wg_copy(src, i):
        return copy(src, wg_recv.at[q_rows(i), :], p_ssem.at[3 + i], p_rsem.at[3 + i], pair)

    def make_near(i, _):
        value = rows_of(z, perm(i))

        @pl.when(i < half)
        def _():
            wg_send[q_rows(i), :] = value
            wg_copy(wg_send.at[q_rows(i), :], i).start()

        @pl.when(i >= half)
        def _():
            wg_ref[q_rows(i - half), cols(y)] = value
        return 0

    def take_far(i, _):
        q = perm(i)
        far_landed(q).wait_recv()

        @pl.when(i < half)
        def _():
            wg_copy(far_recv.at[q_rows(q), :], i).start()

        @pl.when(i >= half)
        def _():
            wg_ref[q_rows(i - half), cols(y)] = far_recv[q_rows(q), :]
        return 0

    order = [L - 1, 0, L - 2, 1]
    for p in range(L):
        g_slot(p, y, x, c)[...] = g_ref[:, p * FB:(p + 1) * FB]
    unit(A, z, y, S)[...] = a_ref[:, cols(y)]
    unit(W, z, y, R)[...] = w_ref[:, cols(y)]
    pl.semaphore_wait(barrier, 2 + nx + has_above.astype(jnp.int32) + has_below.astype(jnp.int32))

    a_swap().start()
    z_all(lambda cp: cp.start())
    spread(order[0], g_slot)
    a_spread(z, y)
    w_swap().start()
    w_out(z, y)
    from_pair(order[0], g_slot)
    spread(order[1], g_slot)
    rest(order[0], g_slot)
    a_copy(z, oy, 0, core).wait_recv()
    a_spread(z, oy)
    w_copy(z, oy, 0, core).wait_recv()
    w_out(z, oy)

    @pl.when(at_end)
    def _():
        for yy in range(2):
            w_in(z, yy)

    @pl.when(middle)
    def _():
        for j in (0, 1):
            z_arrived(extra_layer(0), j)
        a_wave(extra_layer(0))
        for yy in range(2):
            w_in(z, yy)

    for i in range(1, L):
        from_pair(order[i], g_slot)
        if i + 1 < L:
            spread(order[i + 1], g_slot)
        rest(order[i], g_slot)

    @pl.when(middle)
    def _():
        for j in (0, 1):
            z_arrived(extra_layer(1), j)
        extra(0)
        for j in (0, 1):
            z_arrived(extra_layer(2), j)
        extra(1)

    acc[...] = jnp.zeros_like(acc)
    attn_block(z)
    w_wave(1)

    @pl.when(middle)
    def _():
        a_wave(extra_layer(1))
        extra(2)
        a_wave(extra_layer(2))
        lax.fori_loop(0, Q, make_far, 0)

    w_wave(2)

    @pl.when(middle)
    def _():
        lax.fori_loop(0, Q, make_near, 0)

    w_wave(3)

    attn_send[...] = acc[pl.ds(pl.multiple_of(oy * S, S), S), :].astype(attn_send.dtype)
    attn_back = copy(attn_send, attn_recv, p_ssem.at[2], p_rsem.at[2], pair)
    attn_back.start()
    attn_ref[:, cols(y)] = acc[pl.ds(pl.multiple_of(y * S, S), S), :].astype(attn_ref.dtype)

    @pl.when(at_end)
    def _():
        lax.fori_loop(0, Q, take_far, 0)

    attn_back.wait_recv()
    attn_ref[:, cols(oy)] = attn_recv[...]

    def back(i, _):
        cp = wg_copy(wg_send.at[q_rows(i), :], i)
        cp.wait_recv()
        wg_ref[q_rows(i), cols(oy)] = wg_recv[q_rows(i), :]
        cp.wait_send()
        return 0

    lax.fori_loop(0, half, back, 0)

    attn_back.wait_send()
    a_swap().wait_send()
    w_swap().wait_send()
    z_all(lambda cp: cp.wait_send())
    for p in range(L):
        all_sent(p, g_slot)

    @pl.when(middle)
    def _():
        def sent(e, _):
            zz = extra_layer(e // 2)
            all_sent(L + zz * 2 + e % 2, gx_slot)
            return 0
        lax.fori_loop(0, 6, sent, 0)

        def far_sent(q, _):
            far_copy(q).wait_send()
            return 0
        lax.fori_loop(0, Q, far_sent, 0)

    def line_sent(b, _):
        for yy in range(2):
            pl.when(jnp.logical_and(has_above, b <= z))(lambda: w_copy(b, yy, 0, above).wait_send())
            pl.when(jnp.logical_and(has_below, b >= z))(lambda: w_copy(b, yy, 1, below).wait_send())
            pl.when(a_up(b))(lambda: a_copy(b, yy, 0, above).wait_send())
            pl.when(a_down(b))(lambda: a_copy(b, yy, 1, below).wait_send())
        return 0

    lax.fori_loop(0, L, line_sent, 0)


def solution(mesh):
    n_dp, n_t = mesh.shape["dp"], mesh.shape["tensor"]
    L, nx = n_dp // 2, n_t // 2

    def body(out_grad, attn_out, o_weight):
        S, C = attn_out.shape
        R = o_weight.shape[0]
        H, FB, K = C // 2, 2 * R, 2 * S
        Q = FB // CHUNK
        dma = pltpu.SemaphoreType.DMA
        bf16, f32 = jnp.bfloat16, jnp.float32
        vmem = pl.BlockSpec(memory_space=pltpu.VMEM)
        def call(body_of, scratch, collective_id):
            return pl.pallas_call(
                body_of,
                out_shape=(jax.ShapeDtypeStruct((S, C), bf16), jax.ShapeDtypeStruct((R, C), f32)),
                in_specs=[vmem] * 3,
                out_specs=(vmem, vmem),
                scratch_shapes=scratch,
                compiler_params=pltpu.CompilerParams(
                    collective_id=collective_id, has_side_effects=True, vmem_limit_bytes=60 * 1024 * 1024),
                cost_estimate=pl.CostEstimate(
                    flops=4 * K * FB * L * H, bytes_accessed=8 * R * C, transcendentals=0),
            )(out_grad, attn_out, o_weight)

        if L == 4 and 2 * K * FB * (L + 2 * L) <= 32 * 1024 * 1024:
            return call(functools.partial(gather_kernel, n_t), [
                pltpu.VMEM((L, K, FB), bf16),
                pltpu.VMEM((2 * L, K, FB), bf16),
                pltpu.VMEM((L, K, H), bf16),
                pltpu.VMEM((L, FB, H), bf16),
                pltpu.VMEM((K, H), f32),
                pltpu.VMEM((S, H), bf16),
                pltpu.VMEM((S, H), bf16),
                pltpu.VMEM((FB, H), f32),
                pltpu.VMEM((FB, H), f32),
                pltpu.VMEM((R, H), f32),
                pltpu.VMEM((R, H), f32),
                dma((3 * L, 4 * nx - 1)),
                dma((3 * L, 4 * nx - 1)),
                dma((4,)),
                dma((2 * L,)),
                dma((2, n_dp)),
                dma((n_dp,)),
                dma((2, n_dp)),
                dma((n_dp,)),
                dma((Q,)),
                dma((Q,)),
                dma((3 + Q // 2,)),
                dma((3 + Q // 2,)),
            ], 1)
        return call(functools.partial(sum_kernel, n_dp, n_t), [
                pltpu.VMEM((L, K, FB), bf16),
                pltpu.VMEM((K, H), bf16),
                pltpu.VMEM((L, FB, H), bf16),
                pltpu.VMEM((L, FB, H), f32),
                pltpu.VMEM((L, FB, H), f32),
                pltpu.VMEM((K, H), f32),
                pltpu.VMEM((S, H), bf16),
                pltpu.VMEM((S, H), bf16),
                pltpu.VMEM((R, H), f32),
                pltpu.VMEM((R, H), f32),
                dma((L, 4 * nx - 1)),
                dma((L, 4 * nx - 1)),
                dma((2, n_dp)),
                dma((n_dp,)),
                dma((2, L, Q)),
                dma((2, L, Q)),
                dma((3 + Q // 2,)),
                dma((3 + Q // 2,)),
        ], 0)

    return jax.shard_map(
        body,
        mesh=mesh,
        in_specs=(P(("dp", "tensor"), None), P("dp", "tensor"), P("dp", "tensor")),
        out_specs=(P("dp", "tensor"), P("dp", "tensor")),
        check_vma=False,
    )
```

```python
import functools

import jax
import jax.numpy as jnp
from jax import lax
from jax.experimental import pallas as pl
from jax.experimental.pallas import tpu as pltpu
from jax.sharding import PartitionSpec as P

MESH = pl.DeviceIdType.MESH
CHUNK = 256


def kernel(n_dp, n_t, g_ref, a_ref, w_ref, attn_ref, wg_ref,
           G, A, W, up, down, acc, attn_send, attn_recv, wg_send, wg_recv,
           g_ssem, g_rsem, w_ssem, w_rsem, rs_ssem, rs_rsem, p_ssem, p_rsem):
    L, nx = n_dp // 2, n_t // 2
    T, S, R = g_ref.shape[0], a_ref.shape[0], w_ref.shape[0]
    H = a_ref.shape[1] // 2
    FB = 2 * R
    Q = FB // CHUNK
    K = 2 * S
    d, t = lax.axis_index("dp"), lax.axis_index("tensor")
    z, y = d // 2, d % 2
    x, c = t // 2, t % 2
    oy = 1 - y
    pair, core = (d + 1 - 2 * y, t), (d, t + 1 - 2 * c)
    above, below = (d + 2, t), (d - 2, t)
    has_above, has_below = z < L - 1, z > 0

    def beside(k):
        return (d, lax.rem(x + k, nx) * 2 + c)

    def cols(half):
        return pl.ds(pl.multiple_of(half * H, H), H)

    def copy(src, dst, ssem, rsem, to):
        return pltpu.make_async_remote_copy(
            src_ref=src, dst_ref=dst, send_sem=ssem, recv_sem=rsem, device_id=to, device_id_type=MESH)

    barrier = pltpu.get_barrier_semaphore()
    for other in [pair, core] + [beside(k) for k in range(1, nx)]:
        pl.semaphore_signal(barrier, inc=1, device_id=other, device_id_type=MESH)

    @pl.when(has_above)
    def _():
        pl.semaphore_signal(barrier, inc=1, device_id=above, device_id_type=MESH)

    @pl.when(has_below)
    def _():
        pl.semaphore_signal(barrier, inc=1, device_id=below, device_id_type=MESH)

    order = [v for s in range((L + 1) // 2) for v in ([L - 1 - s, s] if s != L - 1 - s else [s])]

    def block_at(p):
        return jnp.where(z < (L + 1) // 2, order[p], L - 1 - order[p])

    def g_slot(b, yy, xx, cc):
        row = pl.multiple_of((yy * n_t + xx * 2 + cc) * T, T)
        return G.at[b, pl.ds(row, T), :]

    def g_copy(p, slot, s_idx, r_idx, to):
        return copy(slot, slot, g_ssem.at[p, s_idx], g_rsem.at[p, r_idx], to)

    def xm(m):
        return lax.rem(x + m, nx)

    def g_own(p):
        b = block_at(p)
        slot = g_slot(b, y, x, c)
        slot[...] = g_ref[:, pl.ds(pl.multiple_of(b * FB, FB), FB)]
        g_copy(p, slot, 0, 0, pair).start()
        for k in range(1, nx):
            g_copy(p, slot, k, nx - k, beside(k)).start()
        g_copy(p, slot, 2 * nx - 1, 2 * nx - 1, core).start()

    def to_core(p, slot, j):
        g_copy(p, slot, 2 * nx - 1 + j, 2 * nx - 1 + j, core).start()

    def g_arrived(p, slot, r_idx):
        g_copy(p, slot, r_idx, r_idx, core).wait_recv()

    def g_from_pair(p):
        slot = g_slot(block_at(p), oy, x, c)
        g_arrived(p, slot, 0)
        for k in range(1, nx):
            g_copy(p, slot, nx - 1 + k, nx - 1 + nx - k, beside(k)).start()
        to_core(p, slot, nx)

    def g_rest(p):
        b = block_at(p)
        for m in range(1, nx):
            slot = g_slot(b, y, xm(m), c)
            g_arrived(p, slot, m)
            to_core(p, slot, m)
        for m in range(1, nx):
            slot = g_slot(b, oy, xm(m), c)
            g_arrived(p, slot, nx - 1 + m)
            to_core(p, slot, nx + m)
        for yy in range(2):
            for m in range(nx):
                slot = g_slot(b, y if yy == 0 else oy, xm(m), 1 - c)
                g_arrived(p, slot, 2 * nx - 1 + yy * nx + m)

    def g_sent(p):
        slot = g_slot(block_at(p), y, x, c)
        for i in range(4 * nx - 1):
            g_copy(p, slot, i, i, core).wait_send()

    def w_slot(b, yy):
        return W.at[b, pl.ds(pl.multiple_of(yy * R, R), R), :]

    def w_copy(b, yy, way, to):
        slot = w_slot(b, yy)
        return copy(slot, slot, w_ssem.at[way, b * 2 + yy], w_rsem.at[b * 2 + yy], to)

    def w_spread(b, yy, upward, downward):
        if upward:
            @pl.when(has_above)
            def _():
                w_copy(b, yy, 0, above).start()
        if downward:
            @pl.when(has_below)
            def _():
                w_copy(b, yy, 1, below).start()

    def a_swap(buf):
        return copy(a_ref.at[:, cols(oy)], buf.at[pl.ds(pl.multiple_of(y * S, S), S), :],
                    p_ssem.at[0], p_rsem.at[0], pair)

    def w_swap():
        return copy(w_ref.at[:, cols(oy)], w_slot(z, y), p_ssem.at[1], w_rsem.at[d], pair)

    def attn_block(b):
        def rows(i, _):
            r = pl.ds(pl.multiple_of(i * 256, 256), 256)
            acc[r, :] += jnp.dot(G[b, r, :], W[b], preferred_element_type=jnp.float32)
            return 0
        lax.fori_loop(0, K // 256, rows, 0)

    def w_wave(h):
        @pl.when(z - h >= 0)
        def _():
            for yy in range(2):
                w_copy(z - h, yy, 0, above).wait_recv()
                w_spread(z - h, yy, True, False)

        @pl.when(z + h <= L - 1)
        def _():
            for yy in range(2):
                w_copy(z + h, yy, 1, below).wait_recv()
                w_spread(z + h, yy, False, True)

    def attn_wave(h):
        @pl.when(z - h >= 0)
        def _():
            attn_block(z - h)

        @pl.when(z + h <= L - 1)
        def _():
            attn_block(z + h)

    def rs_rows(q):
        return pl.ds(pl.multiple_of(q * CHUNK, CHUNK), CHUNK)

    def rs_copy(buf, way, b, q, to):
        slot = buf.at[b, rs_rows(q), :]
        return copy(slot, slot, rs_ssem.at[way, b, q], rs_rsem.at[way, b, q], to)

    def part(b, q):
        return lax.dot_general(G[b, :, rs_rows(q)], A[...], (((0,), (0,)), ((), ())),
                               preferred_element_type=jnp.float32)

    def rs_step(buf, way, b, q, has_before, to):
        buf_part = part(b, q)

        @pl.when(has_before)
        def _():
            rs_copy(buf, way, b, q, to).wait_recv()
            buf[b, rs_rows(q), :] += buf_part

        @pl.when(jnp.logical_not(has_before))
        def _():
            buf[b, rs_rows(q), :] = buf_part

        rs_copy(buf, way, b, q, to).start()

    def perm(i):
        return lax.rem(i + oy * (Q // 2), Q)

    def rs_iter(i):
        ui, di = i - z, i - (L - 1 - z)
        uc, dc = jnp.maximum(ui, 0), jnp.maximum(di, 0)

        @pl.when(jnp.logical_and(ui >= 0, ui < (L - 1 - z) * Q))
        def _():
            rs_step(up, 0, L - 1 - uc // Q, perm(lax.rem(uc, Q)), has_below, above)

        @pl.when(jnp.logical_and(di >= 0, di < z * Q))
        def _():
            rs_step(down, 1, dc // Q, perm(lax.rem(dc, Q)), has_above, below)

    def rs_stage(s):
        def one(i, _):
            rs_iter(i)
            return 0
        lax.fori_loop(s * Q, (s + 1) * Q, one, 0)

    acc[...] = jnp.zeros_like(acc)
    A[pl.ds(pl.multiple_of(y * S, S), S), :] = a_ref[:, cols(y)]
    w_slot(z, y)[...] = w_ref[:, cols(y)]
    pl.semaphore_wait(barrier, 1 + nx + has_above.astype(jnp.int32) + has_below.astype(jnp.int32))

    a_swap(A).start()
    g_own(0)
    w_spread(z, y, True, True)
    g_from_pair(0)
    w_swap().start()
    for p in range(1, min(L, 3)):
        g_own(p)
    g_rest(0)
    a_swap(A).wait_recv()
    at_end = jnp.logical_or(z == 0, z == L - 1)

    @pl.when(at_end)
    def _():
        rs_stage(0)

    if L > 1:
        g_from_pair(1)
    w_copy(z, oy, 0, above).wait_recv()
    w_spread(z, oy, True, True)
    for p in range(3, L):
        g_own(p)
    for p in range(2, L):
        g_from_pair(p)
    for p in range(1, L):
        g_rest(p)

    @pl.when(jnp.logical_not(at_end))
    def _():
        rs_stage(0)

    for s in range(1, L):
        w_wave(s)
        if s < L - 1:
            rs_stage(s)
        if s == 1:
            attn_block(z)
        attn_wave(s)

    other_rows = pl.ds(pl.multiple_of(oy * S, S), S)
    own_rows = pl.ds(pl.multiple_of(y * S, S), S)
    attn_send[...] = acc[other_rows, :].astype(attn_send.dtype)
    attn_back = copy(attn_send, attn_recv, p_ssem.at[2], p_rsem.at[2], pair)
    attn_back.start()
    attn_ref[:, cols(y)] = acc[own_rows, :].astype(attn_ref.dtype)

    def wg_copy(i):
        r = rs_rows(i)
        return copy(wg_send.at[r, :], wg_recv.at[r, :], p_ssem.at[3 + i], p_rsem.at[3 + i], pair)

    def last(i, _):
        half = Q // 2
        q = perm(i)
        total = part(z, q)
        acc[rs_rows(0), :] = total

        @pl.when(has_below)
        def _():
            rs_copy(up, 0, z, q, above).wait_recv()
            acc[rs_rows(0), :] += up[z, rs_rows(q), :]

        @pl.when(has_above)
        def _():
            rs_copy(down, 1, z, q, below).wait_recv()
            acc[rs_rows(0), :] += down[z, rs_rows(q), :]

        @pl.when(i < half)
        def _():
            wg_send[rs_rows(i), :] = acc[rs_rows(0), :]
            wg_copy(i).start()

        @pl.when(i >= half)
        def _():
            wg_ref[rs_rows(i - half), cols(y)] = acc[rs_rows(0), :]
        return 0

    lax.fori_loop(0, Q, last, 0)
    attn_back.wait_recv()
    attn_ref[:, cols(oy)] = attn_recv[...]

    def back(i, _):
        wg_copy(i).wait_recv()
        wg_ref[rs_rows(i), cols(oy)] = wg_recv[rs_rows(i), :]
        wg_copy(i).wait_send()
        return 0

    lax.fori_loop(0, Q // 2, back, 0)

    attn_back.wait_send()
    a_swap(A).wait_send()
    w_swap().wait_send()
    for p in range(L):
        g_sent(p)

    def w_sent(b, _):
        for yy in range(2):
            @pl.when(jnp.logical_and(has_above, b <= z))
            def _():
                w_copy(b, yy, 0, above).wait_send()

            @pl.when(jnp.logical_and(has_below, b >= z))
            def _():
                w_copy(b, yy, 1, below).wait_send()

        def chunk(q, _):
            @pl.when(b > z)
            def _():
                rs_copy(up, 0, b, q, above).wait_send()

            @pl.when(b < z)
            def _():
                rs_copy(down, 1, b, q, below).wait_send()
            return 0
        lax.fori_loop(0, Q, chunk, 0)
        return 0

    lax.fori_loop(0, L, w_sent, 0)


def solution(mesh):
    n_dp, n_t = mesh.shape["dp"], mesh.shape["tensor"]
    L, nx = n_dp // 2, n_t // 2

    def body(out_grad, attn_out, o_weight):
        S, C = attn_out.shape
        R = o_weight.shape[0]
        H, FB, K = C // 2, 2 * R, 2 * S
        Q = FB // CHUNK
        dma = pltpu.SemaphoreType.DMA
        bf16, f32 = jnp.bfloat16, jnp.float32
        vmem = pl.BlockSpec(memory_space=pltpu.VMEM)
        return pl.pallas_call(
            functools.partial(kernel, n_dp, n_t),
            out_shape=(jax.ShapeDtypeStruct((S, C), bf16), jax.ShapeDtypeStruct((R, C), f32)),
            in_specs=[vmem] * 3,
            out_specs=(vmem, vmem),
            scratch_shapes=[
                pltpu.VMEM((L, K, FB), bf16),
                pltpu.VMEM((K, H), bf16),
                pltpu.VMEM((L, FB, H), bf16),
                pltpu.VMEM((L, FB, H), f32),
                pltpu.VMEM((L, FB, H), f32),
                pltpu.VMEM((K, H), f32),
                pltpu.VMEM((S, H), bf16),
                pltpu.VMEM((S, H), bf16),
                pltpu.VMEM((R, H), f32),
                pltpu.VMEM((R, H), f32),
                dma((L, 4 * nx - 1)),
                dma((L, 4 * nx - 1)),
                dma((2, n_dp)),
                dma((n_dp,)),
                dma((2, L, Q)),
                dma((2, L, Q)),
                dma((3 + Q // 2,)),
                dma((3 + Q // 2,)),
            ],
            compiler_params=pltpu.CompilerParams(
                collective_id=0, has_side_effects=True, vmem_limit_bytes=60 * 1024 * 1024),
            cost_estimate=pl.CostEstimate(
                flops=4 * K * FB * L * H, bytes_accessed=8 * R * C, transcendentals=0),
        )(out_grad, attn_out, o_weight)

    return jax.shard_map(
        body,
        mesh=mesh,
        in_specs=(P(("dp", "tensor"), None), P("dp", "tensor"), P("dp", "tensor")),
        out_specs=(P("dp", "tensor"), P("dp", "tensor")),
        check_vma=False,
    )
```

```python
import functools

import jax
import jax.numpy as jnp
from jax import lax
from jax.experimental import pallas as pl
from jax.experimental.pallas import tpu as pltpu
from jax.sharding import PartitionSpec as P

MESH = pl.DeviceIdType.MESH
CHUNK = 256


def kernel(n_dp, n_t, g_ref, a_ref, w_ref, attn_ref, wg_ref,
           G, A, W, up, down, acc, attn_send, attn_recv, wg_send, wg_recv,
           g_ssem, g_rsem, w_ssem, w_rsem, rs_ssem, rs_rsem, p_ssem, p_rsem, e_ssem, e_rsem):
    L, nx = n_dp // 2, n_t // 2
    T, S, R = g_ref.shape[0], a_ref.shape[0], w_ref.shape[0]
    H = a_ref.shape[1] // 2
    FB = 2 * R
    Q = FB // CHUNK
    K = 2 * S
    d, t = lax.axis_index("dp"), lax.axis_index("tensor")
    z, y = d // 2, d % 2
    x, c = t // 2, t % 2
    oy = 1 - y
    pair, core = (d + 1 - 2 * y, t), (d, t + 1 - 2 * c)
    above, below = (d + 2, t), (d - 2, t)
    has_above, has_below = z < L - 1, z > 0
    at_end = jnp.logical_or(z == 0, z == L - 1)
    by_low, by_high = z == 1, z == L - 2
    by_end = jnp.logical_or(by_low, by_high)
    neighbour = (jnp.where(z == 0, d + 2, d - 2), t)
    sums_up = jnp.where(z == 0, L - 2, L - 1 - z)
    sums_down = jnp.where(z == L - 1, L - 2, z)

    def beside(k):
        return (d, lax.rem(x + k, nx) * 2 + c)

    def cols(half):
        return pl.ds(pl.multiple_of(half * H, H), H)

    def copy(src, dst, ssem, rsem, to):
        return pltpu.make_async_remote_copy(
            src_ref=src, dst_ref=dst, send_sem=ssem, recv_sem=rsem, device_id=to, device_id_type=MESH)

    barrier = pltpu.get_barrier_semaphore()
    for other in [pair, core] + [beside(k) for k in range(1, nx)]:
        pl.semaphore_signal(barrier, inc=1, device_id=other, device_id_type=MESH)

    @pl.when(has_above)
    def _():
        pl.semaphore_signal(barrier, inc=1, device_id=above, device_id_type=MESH)

    @pl.when(has_below)
    def _():
        pl.semaphore_signal(barrier, inc=1, device_id=below, device_id_type=MESH)

    order = [v for s in range((L + 1) // 2) for v in ([L - 1 - s, s] if s != L - 1 - s else [s])]

    def block_at(p):
        if p == L:
            return L
        return jnp.where(z < (L + 1) // 2, order[p], L - 1 - order[p])

    def g_slot(b, yy, xx, cc):
        row = pl.multiple_of((yy * n_t + xx * 2 + cc) * T, T)
        return G.at[b, pl.ds(row, T), :]

    def g_copy(p, slot, s_idx, r_idx, to):
        return copy(slot, slot, g_ssem.at[p, s_idx], g_rsem.at[p, r_idx], to)

    def xm(m):
        return lax.rem(x + m, nx)

    def g_own(p):
        b = block_at(p)
        slot = g_slot(b, y, x, c)
        slot[...] = g_ref[:, pl.ds(pl.multiple_of(b * FB, FB), FB)]
        g_spread(p, slot)

    def g_spread(p, slot):
        g_copy(p, slot, 0, 0, pair).start()
        for k in range(1, nx):
            g_copy(p, slot, k, nx - k, beside(k)).start()
        g_copy(p, slot, 2 * nx - 1, 2 * nx - 1, core).start()

    def to_core(p, slot, j):
        g_copy(p, slot, 2 * nx - 1 + j, 2 * nx - 1 + j, core).start()

    def g_arrived(p, slot, r_idx):
        g_copy(p, slot, r_idx, r_idx, core).wait_recv()

    def g_from_pair(p):
        slot = g_slot(block_at(p), oy, x, c)
        g_arrived(p, slot, 0)
        for k in range(1, nx):
            g_copy(p, slot, nx - 1 + k, nx - 1 + nx - k, beside(k)).start()
        to_core(p, slot, nx)

    def g_rest(p):
        b = block_at(p)
        for m in range(1, nx):
            slot = g_slot(b, y, xm(m), c)
            g_arrived(p, slot, m)
            to_core(p, slot, m)
        for m in range(1, nx):
            slot = g_slot(b, oy, xm(m), c)
            g_arrived(p, slot, nx - 1 + m)
            to_core(p, slot, nx + m)
        for yy in range(2):
            for m in range(nx):
                slot = g_slot(b, y if yy == 0 else oy, xm(m), 1 - c)
                g_arrived(p, slot, 2 * nx - 1 + yy * nx + m)

    def g_sent(p):
        slot = g_slot(block_at(p), y, x, c)
        for i in range(4 * nx - 1):
            g_copy(p, slot, i, i, core).wait_send()

    def w_slot(b, yy):
        return W.at[b, pl.ds(pl.multiple_of(yy * R, R), R), :]

    def w_copy(b, yy, way, to):
        slot = w_slot(b, yy)
        return copy(slot, slot, w_ssem.at[way, b * 2 + yy], w_rsem.at[b * 2 + yy], to)

    def w_spread(b, yy, upward, downward):
        if upward:
            @pl.when(has_above)
            def _():
                w_copy(b, yy, 0, above).start()
        if downward:
            @pl.when(has_below)
            def _():
                w_copy(b, yy, 1, below).start()

    def a_slot(i, yy):
        return A.at[i, pl.ds(pl.multiple_of(yy * S, S), S), :]

    def a_swap():
        return copy(a_ref.at[:, cols(oy)], a_slot(0, y),
                    p_ssem.at[0], p_rsem.at[0], pair)

    def end_copy(i):
        if i == 2:
            b = jnp.where(z == 0, 1, L - 2)
            src = g_ref.at[:, pl.ds(pl.multiple_of(b * FB, FB), FB)]
            dst = g_slot(L, y, x, c)
        else:
            yy = y if i == 0 else oy
            src, dst = a_slot(0, yy), a_slot(1, yy)
        return copy(src, dst, e_ssem.at[i], e_rsem.at[i], neighbour)

    def w_swap():
        return copy(w_ref.at[:, cols(oy)], w_slot(z, y), p_ssem.at[1], w_rsem.at[d], pair)

    def attn_block(b):
        def rows(i, _):
            r = pl.ds(pl.multiple_of(i * 256, 256), 256)
            acc[r, :] += jnp.dot(G[b, r, :], W[b], preferred_element_type=jnp.float32)
            return 0
        lax.fori_loop(0, K // 256, rows, 0)

    def w_wave(h):
        @pl.when(z - h >= 0)
        def _():
            for yy in range(2):
                w_copy(z - h, yy, 0, above).wait_recv()
                w_spread(z - h, yy, True, False)

        @pl.when(z + h <= L - 1)
        def _():
            for yy in range(2):
                w_copy(z + h, yy, 1, below).wait_recv()
                w_spread(z + h, yy, False, True)

    def attn_wave(h):
        @pl.when(z - h >= 0)
        def _():
            attn_block(z - h)

        @pl.when(z + h <= L - 1)
        def _():
            attn_block(z + h)

    def rs_rows(q):
        return pl.ds(pl.multiple_of(q * CHUNK, CHUNK), CHUNK)

    def rs_copy(buf, way, b, q, to):
        slot = buf.at[b, rs_rows(q), :]
        return copy(slot, slot, rs_ssem.at[way, b, q], rs_rsem.at[way, b, q], to)

    def part(b, q, i=0):
        return lax.dot_general(G[b, :, rs_rows(q)], A[i], (((0,), (0,)), ((), ())),
                               preferred_element_type=jnp.float32)

    def rs_step(buf, way, b, q, has_before, to):
        buf_part = part(b, q)

        @pl.when(has_before)
        def _():
            rs_copy(buf, way, b, q, to).wait_recv()
            buf[b, rs_rows(q), :] += buf_part

        @pl.when(jnp.logical_not(has_before))
        def _():
            buf[b, rs_rows(q), :] = buf_part

        rs_copy(buf, way, b, q, to).start()

    def perm(i):
        return lax.rem(i + oy * (Q // 2), Q)

    def rs_iter(i):
        ui, di = i - z, i - (L - 1 - z)
        uc, dc = jnp.maximum(ui, 0), jnp.maximum(di, 0)

        @pl.when(jnp.logical_and(ui >= 0, ui < sums_up * Q))
        def _():
            rs_step(up, 0, L - 1 - uc // Q, perm(lax.rem(uc, Q)), has_below, above)

        @pl.when(jnp.logical_and(di >= 0, di < sums_down * Q))
        def _():
            rs_step(down, 1, dc // Q, perm(lax.rem(dc, Q)), has_above, below)

    def rs_stage(s):
        def one(i, _):
            rs_iter(i)
            return 0
        lax.fori_loop(s * Q, (s + 1) * Q, one, 0)

    acc[...] = jnp.zeros_like(acc)
    a_slot(0, y)[...] = a_ref[:, cols(y)]
    w_slot(z, y)[...] = w_ref[:, cols(y)]
    pl.semaphore_wait(barrier, 1 + nx + has_above.astype(jnp.int32) + has_below.astype(jnp.int32))

    a_swap().start()
    g_own(0)
    w_spread(z, y, True, True)

    @pl.when(at_end)
    def _():
        end_copy(2).start()
        end_copy(0).start()

    g_from_pair(0)
    w_swap().start()
    for p in range(1, min(L, 3)):
        g_own(p)
    g_rest(0)
    a_swap().wait_recv()

    @pl.when(at_end)
    def _():
        rs_stage(0)
        end_copy(1).start()

    if L > 1:
        g_from_pair(1)
    w_copy(z, oy, 0, above).wait_recv()
    w_spread(z, oy, True, True)
    for p in range(3, L):
        g_own(p)
    for p in range(2, L):
        g_from_pair(p)

    @pl.when(by_end)
    def _():
        end_copy(2).wait_recv()
        g_spread(L, g_slot(L, y, x, c))

    for p in range(1, L):
        g_rest(p)

    @pl.when(by_end)
    def _():
        g_from_pair(L)

    @pl.when(jnp.logical_not(at_end))
    def _():
        rs_stage(0)

    @pl.when(by_end)
    def _():
        g_rest(L)

    for s in range(1, L):
        w_wave(s)
        if s < L - 1:
            rs_stage(s)
        if s == 1:
            attn_block(z)
        attn_wave(s)

    other_rows = pl.ds(pl.multiple_of(oy * S, S), S)
    own_rows = pl.ds(pl.multiple_of(y * S, S), S)
    attn_send[...] = acc[other_rows, :].astype(attn_send.dtype)
    attn_back = copy(attn_send, attn_recv, p_ssem.at[2], p_rsem.at[2], pair)
    attn_back.start()
    attn_ref[:, cols(y)] = acc[own_rows, :].astype(attn_ref.dtype)

    def wg_copy(i):
        r = rs_rows(i)
        return copy(wg_send.at[r, :], wg_recv.at[r, :], p_ssem.at[3 + i], p_rsem.at[3 + i], pair)

    def last(i, _):
        half = Q // 2
        q = perm(i)
        total = part(z, q)
        acc[rs_rows(0), :] = total

        @pl.when(by_end)
        def _():
            acc[rs_rows(0), :] += part(L, q, 1)

        @pl.when(jnp.logical_and(has_below, jnp.logical_not(by_low)))
        def _():
            rs_copy(up, 0, z, q, above).wait_recv()
            acc[rs_rows(0), :] += up[z, rs_rows(q), :]

        @pl.when(jnp.logical_and(has_above, jnp.logical_not(by_high)))
        def _():
            rs_copy(down, 1, z, q, below).wait_recv()
            acc[rs_rows(0), :] += down[z, rs_rows(q), :]

        @pl.when(i < half)
        def _():
            wg_send[rs_rows(i), :] = acc[rs_rows(0), :]
            wg_copy(i).start()

        @pl.when(i >= half)
        def _():
            wg_ref[rs_rows(i - half), cols(y)] = acc[rs_rows(0), :]
        return 0

    @pl.when(by_end)
    def _():
        end_copy(0).wait_recv()
        end_copy(1).wait_recv()

    lax.fori_loop(0, Q, last, 0)
    attn_back.wait_recv()
    attn_ref[:, cols(oy)] = attn_recv[...]

    def back(i, _):
        wg_copy(i).wait_recv()
        wg_ref[rs_rows(i), cols(oy)] = wg_recv[rs_rows(i), :]
        wg_copy(i).wait_send()
        return 0

    lax.fori_loop(0, Q // 2, back, 0)

    attn_back.wait_send()
    a_swap().wait_send()
    w_swap().wait_send()
    for p in range(L):
        g_sent(p)

    @pl.when(by_end)
    def _():
        g_sent(L)

    @pl.when(at_end)
    def _():
        for i in range(3):
            end_copy(i).wait_send()

    def w_sent(b, _):
        for yy in range(2):
            @pl.when(jnp.logical_and(has_above, b <= z))
            def _():
                w_copy(b, yy, 0, above).wait_send()

            @pl.when(jnp.logical_and(has_below, b >= z))
            def _():
                w_copy(b, yy, 1, below).wait_send()

        def chunk(q, _):
            @pl.when(b >= L - sums_up)
            def _():
                rs_copy(up, 0, b, q, above).wait_send()

            @pl.when(b < sums_down)
            def _():
                rs_copy(down, 1, b, q, below).wait_send()
            return 0
        lax.fori_loop(0, Q, chunk, 0)
        return 0

    lax.fori_loop(0, L, w_sent, 0)


def solution(mesh):
    n_dp, n_t = mesh.shape["dp"], mesh.shape["tensor"]
    L, nx = n_dp // 2, n_t // 2

    def body(out_grad, attn_out, o_weight):
        S, C = attn_out.shape
        R = o_weight.shape[0]
        H, FB, K = C // 2, 2 * R, 2 * S
        Q = FB // CHUNK
        dma = pltpu.SemaphoreType.DMA
        bf16, f32 = jnp.bfloat16, jnp.float32
        vmem = pl.BlockSpec(memory_space=pltpu.VMEM)
        return pl.pallas_call(
            functools.partial(kernel, n_dp, n_t),
            out_shape=(jax.ShapeDtypeStruct((S, C), bf16), jax.ShapeDtypeStruct((R, C), f32)),
            in_specs=[vmem] * 3,
            out_specs=(vmem, vmem),
            scratch_shapes=[
                pltpu.VMEM((L + 1, K, FB), bf16),
                pltpu.VMEM((2, K, H), bf16),
                pltpu.VMEM((L, FB, H), bf16),
                pltpu.VMEM((L, FB, H), f32),
                pltpu.VMEM((L, FB, H), f32),
                pltpu.VMEM((K, H), f32),
                pltpu.VMEM((S, H), bf16),
                pltpu.VMEM((S, H), bf16),
                pltpu.VMEM((R, H), f32),
                pltpu.VMEM((R, H), f32),
                dma((L + 1, 4 * nx - 1)),
                dma((L + 1, 4 * nx - 1)),
                dma((2, n_dp)),
                dma((n_dp,)),
                dma((2, L, Q)),
                dma((2, L, Q)),
                dma((3 + Q // 2,)),
                dma((3 + Q // 2,)),
                dma((3,)),
                dma((3,)),
            ],
            compiler_params=pltpu.CompilerParams(
                collective_id=0, has_side_effects=True, vmem_limit_bytes=60 * 1024 * 1024),
            cost_estimate=pl.CostEstimate(
                flops=4 * K * FB * L * H, bytes_accessed=8 * R * C, transcendentals=0),
        )(out_grad, attn_out, o_weight)

    return jax.shard_map(
        body,
        mesh=mesh,
        in_specs=(P(("dp", "tensor"), None), P("dp", "tensor"), P("dp", "tensor")),
        out_specs=(P("dp", "tensor"), P("dp", "tensor")),
        check_vma=False,
    )
```

```python
import functools

import jax
import jax.numpy as jnp
from jax import lax
from jax.experimental import pallas as pl
from jax.experimental.pallas import tpu as pltpu
from jax.sharding import PartitionSpec as P

MESH = pl.DeviceIdType.MESH
CHUNK = 256


def kernel(n_dp, n_t, g_ref, a_ref, w_ref, attn_ref, wg_ref,
           G, A, W, up, down, acc, attn_send, attn_recv, wg_send, wg_recv,
           g_ssem, g_rsem, w_ssem, w_rsem, rs_ssem, rs_rsem, p_ssem, p_rsem):
    L, nx = n_dp // 2, n_t // 2
    T, S, R = g_ref.shape[0], a_ref.shape[0], w_ref.shape[0]
    H = a_ref.shape[1] // 2
    FB = 2 * R
    Q = FB // CHUNK
    K = 2 * S
    d, t = lax.axis_index("dp"), lax.axis_index("tensor")
    z, y = d // 2, d % 2
    x, c = t // 2, t % 2
    oy = 1 - y
    pair, core = (d + 1 - 2 * y, t), (d, t + 1 - 2 * c)
    above, below = (d + 2, t), (d - 2, t)
    has_above, has_below = z < L - 1, z > 0

    def beside(k):
        return (d, lax.rem(x + k, nx) * 2 + c)

    def cols(half):
        return pl.ds(pl.multiple_of(half * H, H), H)

    def copy(src, dst, ssem, rsem, to):
        return pltpu.make_async_remote_copy(
            src_ref=src, dst_ref=dst, send_sem=ssem, recv_sem=rsem, device_id=to, device_id_type=MESH)

    barrier = pltpu.get_barrier_semaphore()
    for other in [pair, core] + [beside(k) for k in range(1, nx)]:
        pl.semaphore_signal(barrier, inc=1, device_id=other, device_id_type=MESH)

    @pl.when(has_above)
    def _():
        pl.semaphore_signal(barrier, inc=1, device_id=above, device_id_type=MESH)

    @pl.when(has_below)
    def _():
        pl.semaphore_signal(barrier, inc=1, device_id=below, device_id_type=MESH)

    order = [v for s in range((L + 1) // 2) for v in ([L - 1 - s, s] if s != L - 1 - s else [s])]

    def block_at(p):
        return jnp.where(z < (L + 1) // 2, order[p], L - 1 - order[p])

    def g_slot(b, yy, xx, cc):
        row = pl.multiple_of((yy * n_t + xx * 2 + cc) * T, T)
        return G.at[b, pl.ds(row, T), :]

    def g_copy(p, slot, s_idx, r_idx, to):
        return copy(slot, slot, g_ssem.at[p, s_idx], g_rsem.at[p, r_idx], to)

    def xm(m):
        return lax.rem(x + m, nx)

    def g_own(p):
        b = block_at(p)
        slot = g_slot(b, y, x, c)
        slot[...] = g_ref[:, pl.ds(pl.multiple_of(b * FB, FB), FB)]
        g_copy(p, slot, 0, 0, pair).start()
        for k in range(1, nx):
            g_copy(p, slot, k, nx - k, beside(k)).start()
        g_copy(p, slot, 2 * nx - 1, 2 * nx - 1, core).start()

    def to_core(p, slot, j):
        g_copy(p, slot, 2 * nx - 1 + j, 2 * nx - 1 + j, core).start()

    def g_arrived(p, slot, r_idx):
        g_copy(p, slot, r_idx, r_idx, core).wait_recv()

    def g_from_pair(p):
        slot = g_slot(block_at(p), oy, x, c)
        g_arrived(p, slot, 0)
        for k in range(1, nx):
            g_copy(p, slot, nx - 1 + k, nx - 1 + nx - k, beside(k)).start()
        to_core(p, slot, nx)

    def g_rest(p):
        b = block_at(p)
        for m in range(1, nx):
            slot = g_slot(b, y, xm(m), c)
            g_arrived(p, slot, m)
            to_core(p, slot, m)
        for m in range(1, nx):
            slot = g_slot(b, oy, xm(m), c)
            g_arrived(p, slot, nx - 1 + m)
            to_core(p, slot, nx + m)
        for yy in range(2):
            for m in range(nx):
                slot = g_slot(b, y if yy == 0 else oy, xm(m), 1 - c)
                g_arrived(p, slot, 2 * nx - 1 + yy * nx + m)

    def g_sent(p):
        slot = g_slot(block_at(p), y, x, c)
        for i in range(4 * nx - 1):
            g_copy(p, slot, i, i, core).wait_send()

    def w_slot(b, yy):
        return W.at[b, pl.ds(pl.multiple_of(yy * R, R), R), :]

    def w_copy(b, yy, way, to):
        slot = w_slot(b, yy)
        return copy(slot, slot, w_ssem.at[way, b * 2 + yy], w_rsem.at[b * 2 + yy], to)

    def w_spread(b, yy, upward, downward):
        if upward:
            @pl.when(has_above)
            def _():
                w_copy(b, yy, 0, above).start()
        if downward:
            @pl.when(has_below)
            def _():
                w_copy(b, yy, 1, below).start()

    def a_swap(buf):
        return copy(a_ref.at[:, cols(oy)], buf.at[pl.ds(pl.multiple_of(y * S, S), S), :],
                    p_ssem.at[0], p_rsem.at[0], pair)

    def w_swap():
        return copy(w_ref.at[:, cols(oy)], w_slot(z, y), p_ssem.at[1], w_rsem.at[d], pair)

    def attn_block(b):
        def rows(i, _):
            r = pl.ds(pl.multiple_of(i * 256, 256), 256)
            acc[r, :] += jnp.dot(G[b, r, :], W[b], preferred_element_type=jnp.float32)
            return 0
        lax.fori_loop(0, K // 256, rows, 0)

    def w_wave(h):
        @pl.when(z - h >= 0)
        def _():
            for yy in range(2):
                w_copy(z - h, yy, 0, above).wait_recv()
                w_spread(z - h, yy, True, False)

        @pl.when(z + h <= L - 1)
        def _():
            for yy in range(2):
                w_copy(z + h, yy, 1, below).wait_recv()
                w_spread(z + h, yy, False, True)

    def attn_wave(h):
        @pl.when(z - h >= 0)
        def _():
            attn_block(z - h)

        @pl.when(z + h <= L - 1)
        def _():
            attn_block(z + h)

    def rs_rows(q):
        return pl.ds(pl.multiple_of(q * CHUNK, CHUNK), CHUNK)

    def rs_copy(buf, way, b, q, to):
        slot = buf.at[b, rs_rows(q), :]
        return copy(slot, slot, rs_ssem.at[way, b, q], rs_rsem.at[way, b, q], to)

    def part(b, q):
        return lax.dot_general(G[b, :, rs_rows(q)], A[...], (((0,), (0,)), ((), ())),
                               preferred_element_type=jnp.float32)

    def rs_step(buf, way, b, q, has_before, to):
        buf_part = part(b, q)

        @pl.when(has_before)
        def _():
            rs_copy(buf, way, b, q, to).wait_recv()
            buf[b, rs_rows(q), :] += buf_part

        @pl.when(jnp.logical_not(has_before))
        def _():
            buf[b, rs_rows(q), :] = buf_part

        rs_copy(buf, way, b, q, to).start()

    def perm(i):
        return lax.rem(i + oy * (Q // 2), Q)

    def rs_iter(i):
        ui, di = i - z, i - (L - 1 - z)
        uc, dc = jnp.maximum(ui, 0), jnp.maximum(di, 0)

        @pl.when(jnp.logical_and(ui >= 0, ui < (L - 1 - z) * Q))
        def _():
            rs_step(up, 0, L - 1 - uc // Q, perm(lax.rem(uc, Q)), has_below, above)

        @pl.when(jnp.logical_and(di >= 0, di < z * Q))
        def _():
            rs_step(down, 1, dc // Q, perm(lax.rem(dc, Q)), has_above, below)

    def rs_stage(s):
        def one(i, _):
            rs_iter(i)
            return 0
        lax.fori_loop(s * Q, (s + 1) * Q, one, 0)

    acc[...] = jnp.zeros_like(acc)
    A[pl.ds(pl.multiple_of(y * S, S), S), :] = a_ref[:, cols(y)]
    w_slot(z, y)[...] = w_ref[:, cols(y)]
    pl.semaphore_wait(barrier, 1 + nx + has_above.astype(jnp.int32) + has_below.astype(jnp.int32))

    a_swap(A).start()
    g_own(0)
    w_spread(z, y, True, True)
    g_from_pair(0)
    w_swap().start()
    for p in range(1, min(L, 3)):
        g_own(p)
    g_rest(0)
    a_swap(A).wait_recv()
    at_end = jnp.logical_or(z == 0, z == L - 1)

    @pl.when(at_end)
    def _():
        rs_stage(0)

    if L > 1:
        g_from_pair(1)
    w_copy(z, oy, 0, above).wait_recv()
    w_spread(z, oy, True, True)
    for p in range(3, L):
        g_own(p)
    for p in range(2, L):
        g_from_pair(p)
    for p in range(1, L):
        g_rest(p)

    if L > 1:
        w_wave(1)

    @pl.when(at_end)
    def _():
        for s in range(1, L - 1):
            rs_stage(s)

    @pl.when(jnp.logical_not(at_end))
    def _():
        rs_stage(0)

    for s in range(2, L):
        w_wave(s)

        @pl.when(jnp.logical_not(at_end))
        def _():
            rs_stage(s - 1)

        if s == 2:
            attn_block(z)
        attn_wave(s - 1)
    if L <= 2:
        attn_block(z)
    if L > 1:
        attn_wave(L - 1)

    other_rows = pl.ds(pl.multiple_of(oy * S, S), S)
    own_rows = pl.ds(pl.multiple_of(y * S, S), S)
    attn_send[...] = acc[other_rows, :].astype(attn_send.dtype)
    attn_back = copy(attn_send, attn_recv, p_ssem.at[2], p_rsem.at[2], pair)
    attn_back.start()
    attn_ref[:, cols(y)] = acc[own_rows, :].astype(attn_ref.dtype)

    def wg_copy(i):
        r = rs_rows(i)
        return copy(wg_send.at[r, :], wg_recv.at[r, :], p_ssem.at[3 + i], p_rsem.at[3 + i], pair)

    def last(i, _):
        half = Q // 2
        q = perm(i)
        total = part(z, q)
        acc[rs_rows(0), :] = total

        @pl.when(has_below)
        def _():
            rs_copy(up, 0, z, q, above).wait_recv()
            acc[rs_rows(0), :] += up[z, rs_rows(q), :]

        @pl.when(has_above)
        def _():
            rs_copy(down, 1, z, q, below).wait_recv()
            acc[rs_rows(0), :] += down[z, rs_rows(q), :]

        @pl.when(i < half)
        def _():
            wg_send[rs_rows(i), :] = acc[rs_rows(0), :]
            wg_copy(i).start()

        @pl.when(i >= half)
        def _():
            wg_ref[rs_rows(i - half), cols(y)] = acc[rs_rows(0), :]
        return 0

    lax.fori_loop(0, Q, last, 0)
    attn_back.wait_recv()
    attn_ref[:, cols(oy)] = attn_recv[...]

    def back(i, _):
        wg_copy(i).wait_recv()
        wg_ref[rs_rows(i), cols(oy)] = wg_recv[rs_rows(i), :]
        wg_copy(i).wait_send()
        return 0

    lax.fori_loop(0, Q // 2, back, 0)

    attn_back.wait_send()
    a_swap(A).wait_send()
    w_swap().wait_send()
    for p in range(L):
        g_sent(p)

    def w_sent(b, _):
        for yy in range(2):
            @pl.when(jnp.logical_and(has_above, b <= z))
            def _():
                w_copy(b, yy, 0, above).wait_send()

            @pl.when(jnp.logical_and(has_below, b >= z))
            def _():
                w_copy(b, yy, 1, below).wait_send()

        def chunk(q, _):
            @pl.when(b > z)
            def _():
                rs_copy(up, 0, b, q, above).wait_send()

            @pl.when(b < z)
            def _():
                rs_copy(down, 1, b, q, below).wait_send()
            return 0
        lax.fori_loop(0, Q, chunk, 0)
        return 0

    lax.fori_loop(0, L, w_sent, 0)


def solution(mesh):
    n_dp, n_t = mesh.shape["dp"], mesh.shape["tensor"]
    L, nx = n_dp // 2, n_t // 2

    def body(out_grad, attn_out, o_weight):
        S, C = attn_out.shape
        R = o_weight.shape[0]
        H, FB, K = C // 2, 2 * R, 2 * S
        Q = FB // CHUNK
        dma = pltpu.SemaphoreType.DMA
        bf16, f32 = jnp.bfloat16, jnp.float32
        vmem = pl.BlockSpec(memory_space=pltpu.VMEM)
        return pl.pallas_call(
            functools.partial(kernel, n_dp, n_t),
            out_shape=(jax.ShapeDtypeStruct((S, C), bf16), jax.ShapeDtypeStruct((R, C), f32)),
            in_specs=[vmem] * 3,
            out_specs=(vmem, vmem),
            scratch_shapes=[
                pltpu.VMEM((L, K, FB), bf16),
                pltpu.VMEM((K, H), bf16),
                pltpu.VMEM((L, FB, H), bf16),
                pltpu.VMEM((L, FB, H), f32),
                pltpu.VMEM((L, FB, H), f32),
                pltpu.VMEM((K, H), f32),
                pltpu.VMEM((S, H), bf16),
                pltpu.VMEM((S, H), bf16),
                pltpu.VMEM((R, H), f32),
                pltpu.VMEM((R, H), f32),
                dma((L, 4 * nx - 1)),
                dma((L, 4 * nx - 1)),
                dma((2, n_dp)),
                dma((n_dp,)),
                dma((2, L, Q)),
                dma((2, L, Q)),
                dma((3 + Q // 2,)),
                dma((3 + Q // 2,)),
            ],
            compiler_params=pltpu.CompilerParams(
                collective_id=0, has_side_effects=True, vmem_limit_bytes=60 * 1024 * 1024),
            cost_estimate=pl.CostEstimate(
                flops=4 * K * FB * L * H, bytes_accessed=8 * R * C, transcendentals=0),
        )(out_grad, attn_out, o_weight)

    return jax.shard_map(
        body,
        mesh=mesh,
        in_specs=(P(("dp", "tensor"), None), P("dp", "tensor"), P("dp", "tensor")),
        out_specs=(P("dp", "tensor"), P("dp", "tensor")),
        check_vma=False,
    )
```
